32 devices in a mesh: date: 4 (over x, core), tile: 4 (over z), col: 2 (over y).
Axes of the slice: x: 2, y: 2, z: 4, core: 2. Of those that a mesh axis runs over, the one named last changes fastest.
Arguments:
- arrivals: bfloat16 [1, 16, 2, 4, 16, 16, 1280], P(None, None, 'col', 'date', 'tile'), may hold values from -24 to 24
- owner_map: int32 [1, 16], replicated, may hold values from 0 to 15, each once within a row
- block_ids: int32 [1, 16, 2], P(None, ('date', 'tile'), 'col'), may hold values from 0 to 15
- tile_valid: int32 [1, 16, 2], P(None, ('date', 'tile'), 'col'), may hold values 0 or 1
- blend_weights: int32 [1, 16, 2, 2, 224], P(None, ('date', 'tile'), 'col'), may hold values from 1 to 8
- location_table: bfloat16 [16, 1280], replicated, may hold values from -3 to 3
- norm_gain: bfloat16 [1280], replicated, may hold values from 0.099609375 to 1.8984375
- qkv_weight: bfloat16 [1280, 3840], replicated, may hold values from -4 to 4
- out_weight: bfloat16 [1280, 1280], replicated, may hold values from -0.3125 to 0.3125
- final_gain: bfloat16 [1280], replicated, may hold values from 0.099609375 to 1.8984375
- reduce_weight: bfloat16 [5120, 256], replicated, may hold values from -0.078125 to 0.078125
- reduce_bias: bfloat16 [256], replicated, may hold values from -3 to 3
- upsample_weight: bfloat16 [256, 3136], replicated, may hold values from -0.375 to 0.375
- class_weight: bfloat16 [9, 13, 16], replicated, may hold values from -1.5 to 1.5
- class_bias: bfloat16 [13], replicated, may hold values from -3 to 3
Outputs:
- composite: float32 [1, 13, 3072, 384], P(None, None, ('date', 'tile'), 'col')
The draws below stay inside these ranges and needn't reach their ends.
Inputs may be any that keep to these rules, and one draw needn't show every extreme that they name: `owner_map`: each scene's row names every tile row of the composite once.
All inputs are finite; a program needn't handle non-finite values. No bound on the sum of `tile_valid` on one device may be relied on, other than what follows from the above.
Results may differ from the reference program's by a relative error of at most 0.009.
Values may be sent and summed in bfloat16 or wider, within the bound.
No kernel may reach another device: no remote copies, remote signals or barrier semaphores. Data moves between devices by JAX's collectives and lax.ppermute only.
A program may use at most 256 MiB of HBM per device.

```python
import math
import jax
import jax.numpy as jnp
from jax import lax

D = 1280
HEADS = 16
DATES = 4
TILE_PX = 224
PATCH = 14
INTERSECTION = 32
DEC = 256
FEAT = 16
NCLS = 13
NBLOCK = 16
SCENES = 1
HEAD_DIM = 80
PATCHES = 16
N_TOK = 1024
RIM = 16
STRIDE = 192
TILE_ROWS = 16
TILE_COLS = 2
MOS_H = 3072
MOS_W = 384


def draw_arrivals(key, part):
    subkeys = jax.random.split(key, 3)
    full_shape = (SCENES, TILE_ROWS, TILE_COLS, DATES, PATCHES, PATCHES, D)
    row_scale = jnp.exp(jax.random.uniform(subkeys[0], full_shape[:-1] + (1,), jnp.float32, 0.0, math.log(10.0))) / 3.0
    column_scale = jnp.exp(jax.random.uniform(subkeys[1], (D,), jnp.float32, 0.0, math.log(10.0))) / 3.0
    values = jnp.clip(jax.random.normal(subkeys[2], full_shape, jnp.float32), -6.0, 6.0)
    return jnp.clip(values * row_scale * column_scale, -24.0, 24.0).astype(jnp.bfloat16)


def draw_qkv_weight(key, part):
    subkeys = jax.random.split(key, 3)
    inverse_root = 1.0 / math.sqrt(D)
    query_part = jnp.clip(jax.random.normal(subkeys[0], (D, D), jnp.float32), -6.0, 6.0) * 1.5 * inverse_root
    noise_part = jnp.clip(jax.random.normal(subkeys[1], (D, D), jnp.float32), -6.0, 6.0)
    value_part = jnp.clip(jax.random.normal(subkeys[2], (D, D), jnp.float32), -6.0, 6.0) * inverse_root
    key_part = 1.5 * inverse_root * noise_part
    return jnp.clip(jnp.concatenate([query_part, key_part, value_part], axis=1), -4.0, 4.0).astype(jnp.bfloat16)


def plant(array, key, least, largest):
    spot = [jax.random.randint(jax.random.fold_in(key, axis), (), 0, length) for axis, length in enumerate(array.shape)]
    main_axis = array.shape.index(max(array.shape))
    next_to = spot[:main_axis] + [(spot[main_axis] + 1) % array.shape[main_axis]] + spot[main_axis + 1:]
    return array.at[tuple(spot)].set(least).at[tuple(next_to)].set(largest)


def normal_values(rng, dims, deviation, reach, kind=jnp.bfloat16):
    entries = jax.random.normal(rng, dims, jnp.float32) * deviation
    return jnp.minimum(jnp.maximum(entries, -reach), reach).astype(kind)


def setup_inputs(seed: int = 0) -> dict:
    seeds = jax.random.split(jax.random.key(seed), 16)
    arrivals = draw_arrivals(jax.random.fold_in(seeds[15], 71), 0)
    owner_map = jax.vmap(lambda own: jax.random.permutation(own, TILE_ROWS))(jax.random.split(seeds[1], SCENES)).reshape((SCENES, TILE_ROWS)).astype(jnp.int32)
    block_ids = plant(jax.random.randint(seeds[2], (SCENES, TILE_ROWS, TILE_COLS), 0, NBLOCK), jax.random.fold_in(seeds[2], 1), 0, NBLOCK - 1).astype(jnp.int32)
    tile_valid = plant((jax.random.randint(seeds[3], (SCENES, TILE_ROWS, TILE_COLS), 0, 4) < 3).astype(jnp.int32), jax.random.fold_in(seeds[3], 1), 0, 1)
    blend_weights = plant(jax.random.randint(seeds[4], (SCENES, TILE_ROWS, TILE_COLS, 2, TILE_PX), 1, 9), jax.random.fold_in(seeds[4], 1), 1, 8).astype(jnp.int32)
    location_table = normal_values(seeds[5], (NBLOCK, D), 0.5, 3.0)
    norm_gain = jnp.clip(1.0 + 0.18 * jax.random.normal(seeds[6], (D,), jnp.float32), 0.099609375, 1.8984375).astype(jnp.bfloat16)
    qkv_weight = draw_qkv_weight(jax.random.fold_in(seeds[15], 71), 0)
    out_weight = normal_values(seeds[8], (D, D), (D // 4) ** -0.5, 0.3125)
    final_gain = jnp.clip(1.0 + 0.18 * jax.random.normal(seeds[9], (D,), jnp.float32), 0.099609375, 1.8984375).astype(jnp.bfloat16)
    reduce_weight = normal_values(seeds[10], (DATES * D, DEC), (DATES * D) ** -0.5, 0.078125)
    reduce_bias = normal_values(seeds[11], (DEC,), 0.5, 3.0)
    upsample_weight = normal_values(seeds[12], (DEC, FEAT * PATCH * PATCH), DEC ** -0.5, 0.375)
    class_weight = normal_values(seeds[13], (9, NCLS, FEAT), FEAT ** -0.5, 1.5)
    class_bias = normal_values(seeds[14], (NCLS,), 1.0, 3.0)
    return dict(arrivals=arrivals, owner_map=owner_map, block_ids=block_ids, tile_valid=tile_valid, blend_weights=blend_weights, location_table=location_table, norm_gain=norm_gain, qkv_weight=qkv_weight, out_weight=out_weight, final_gain=final_gain, reduce_weight=reduce_weight, reduce_bias=reduce_bias, upsample_weight=upsample_weight, class_weight=class_weight, class_bias=class_bias)


norm_eps = 1e-06

def layer_norm(values, gain_row):
    average = lax.optimization_barrier(jnp.mean(values, axis=-1, keepdims=True))
    centered = values - average
    spread = lax.optimization_barrier(jnp.mean(centered * centered, axis=-1, keepdims=True))
    return centered * lax.rsqrt(spread + norm_eps) * gain_row.astype(jnp.float32)

def encode_tile(tokens, location, norm_gain, qkv_weight, out_weight, final_gain):
    residual = tokens.astype(jnp.float32) + location[None, :]
    normed = layer_norm(residual, norm_gain).astype(jnp.bfloat16)
    packed = jnp.dot(normed, qkv_weight, preferred_element_type=jnp.float32).astype(jnp.bfloat16)
    queries = packed[:, :D].reshape(N_TOK, HEADS, HEAD_DIM).astype(jnp.float32)
    key_rows = packed[:, D:2 * D].reshape(N_TOK, HEADS, HEAD_DIM).astype(jnp.float32)
    value_rows = packed[:, 2 * D:].reshape(N_TOK, HEADS, HEAD_DIM).astype(jnp.float32)
    score_scale = 1.0 / math.sqrt(HEAD_DIM)

    def attend(query_block):
        scores = jnp.einsum('qhd,khd->hqk', query_block, key_rows) * score_scale
        highest = lax.optimization_barrier(jnp.max(scores, axis=-1, keepdims=True))
        lifted = jnp.exp(scores - highest)
        attention = (lifted / lax.optimization_barrier(jnp.sum(lifted, axis=-1, keepdims=True))).astype(jnp.bfloat16)
        return jnp.einsum('hqk,khd->qhd', attention.astype(jnp.float32), value_rows).astype(jnp.bfloat16)
    mixed_rows = lax.map(attend, queries.reshape(N_TOK // 512, 512, HEADS, HEAD_DIM)).reshape(N_TOK, D)
    updated = residual + jnp.dot(mixed_rows, out_weight, preferred_element_type=jnp.float32)
    return layer_norm(updated, final_gain).astype(jnp.bfloat16)

def decode_tile(encoded, reduce_weight, reduce_bias, upsample_weight):
    by_date = encoded.reshape(DATES, PATCHES * PATCHES, D).astype(jnp.float32)
    weight_by_date = reduce_weight.reshape(DATES, D, DEC).astype(jnp.float32)
    summed = jnp.einsum('tpd,tdc->pc', by_date, weight_by_date) + reduce_bias.astype(jnp.float32)
    reduced = jax.nn.gelu(summed, approximate=False).astype(jnp.bfloat16)
    upsampled = jnp.dot(reduced, upsample_weight, preferred_element_type=jnp.float32).astype(jnp.bfloat16)
    pixels = upsampled.reshape(PATCHES, PATCHES, FEAT, PATCH, PATCH).transpose(2, 0, 3, 1, 4)
    return pixels.reshape(FEAT, TILE_PX, TILE_PX)

def classify_tile(framed_tile, class_weight, class_bias):
    total = jnp.zeros((NCLS, TILE_PX, TILE_PX), jnp.float32) + class_bias.astype(jnp.float32)[:, None, None]
    framed_float = framed_tile.astype(jnp.float32)
    for offset in range(9):
        row_off = offset // 3
        col_off = offset % 3
        window = framed_float[:, row_off:row_off + TILE_PX, col_off:col_off + TILE_PX]
        total = total + jnp.einsum('kf,fhw->khw', class_weight[offset].astype(jnp.float32), window)
    return total

def shift_forward(values, axis):
    filler = jnp.zeros_like(lax.slice_in_dim(values, 0, 1, axis=axis))
    return jnp.concatenate([filler, lax.slice_in_dim(values, 0, values.shape[axis] - 1, axis=axis)], axis=axis)

def shift_backward(values, axis):
    filler = jnp.zeros_like(lax.slice_in_dim(values, 0, 1, axis=axis))
    return jnp.concatenate([lax.slice_in_dim(values, 1, values.shape[axis], axis=axis), filler], axis=axis)

def fold_tiles(values, tile_axis, pixel_axis):
    main_part = lax.slice_in_dim(values, RIM, RIM + STRIDE, axis=pixel_axis)
    upper_rim = shift_forward(lax.slice_in_dim(values, STRIDE + RIM, TILE_PX, axis=pixel_axis), tile_axis)
    lower_rim = shift_backward(lax.slice_in_dim(values, 0, RIM, axis=pixel_axis), tile_axis)
    filler = jnp.zeros_like(lax.slice_in_dim(main_part, 0, STRIDE - RIM, axis=pixel_axis))
    return main_part + jnp.concatenate([upper_rim, filler], axis=pixel_axis) + jnp.concatenate([filler, lower_rim], axis=pixel_axis)

def reference(arrivals, owner_map, block_ids, tile_valid, blend_weights, location_table, norm_gain, qkv_weight, out_weight, final_gain, reduce_weight, reduce_bias, upsample_weight, class_weight, class_bias):
    arrival_order = jnp.argsort(owner_map, axis=1).astype(jnp.int32)
    ordered = jax.vmap(lambda scene_rows, scene_order: jnp.take(scene_rows, scene_order, axis=0))(arrivals, arrival_order)
    tile_count = SCENES * TILE_ROWS * TILE_COLS
    tile_tokens = ordered.reshape(tile_count, N_TOK, D)
    locations = jnp.take(location_table, block_ids.reshape(-1).astype(jnp.int32), axis=0).astype(jnp.float32)

    def per_tile(inputs):
        tokens, location = inputs
        encoded = encode_tile(tokens, location, norm_gain, qkv_weight, out_weight, final_gain)
        return decode_tile(encoded, reduce_weight, reduce_bias, upsample_weight)
    features = lax.map(per_tile, (tile_tokens, locations))
    grid = features.reshape(SCENES, TILE_ROWS, TILE_COLS, FEAT, TILE_PX, TILE_PX)
    far_edge = TILE_PX - INTERSECTION - 1
    above = shift_forward(lax.slice_in_dim(grid, far_edge, far_edge + 1, axis=4), 1)
    below = shift_backward(lax.slice_in_dim(grid, INTERSECTION, INTERSECTION + 1, axis=4), 1)
    tall = jnp.concatenate([above, grid, below], axis=4)
    left_side = shift_forward(lax.slice_in_dim(tall, far_edge, far_edge + 1, axis=5), 2)
    right_side = shift_backward(lax.slice_in_dim(tall, INTERSECTION, INTERSECTION + 1, axis=5), 2)
    padded = jnp.concatenate([left_side, tall, right_side], axis=5)
    logits = lax.map(lambda framed_tile: classify_tile(framed_tile, class_weight, class_bias), padded.reshape(tile_count, FEAT, TILE_PX + 2, TILE_PX + 2))
    logits = logits.reshape(SCENES, TILE_ROWS, TILE_COLS, NCLS, TILE_PX, TILE_PX)
    profiles = blend_weights.astype(jnp.float32)
    plane = tile_valid.astype(jnp.float32)[:, :, :, None, None] * profiles[:, :, :, 0, :, None] * profiles[:, :, :, 1, None, :]
    numerator = logits * plane[:, :, :, None]
    denominator = plane[:, :, :, None]
    numerator = fold_tiles(fold_tiles(numerator, 1, 4), 2, 5)
    denominator = fold_tiles(fold_tiles(denominator, 1, 4), 2, 5)
    blocks = numerator / jnp.maximum(denominator, 1.0)
    return blocks.transpose(0, 3, 1, 4, 2, 5).reshape(SCENES, NCLS, MOS_H, MOS_W)
```

```python
import functools
import math

import jax
import jax.numpy as jnp
import numpy as np
from jax import lax
from jax.experimental import pallas as pl
from jax.experimental.pallas import tpu as pltpu
from jax.sharding import PartitionSpec as P

HEADS = 16
DATES = 4
PATCH = 14
INTERSECTION = 32
FEAT = 16
PATCHES = 16
RIM = 16
TILE_PX = PATCH * PATCHES
STRIDE = TILE_PX - INTERSECTION
SPAN = PATCH + 2
FAR_PATCH, FAR_PIXEL = divmod(STRIDE - 1, PATCH)
NEAR_PATCH, NEAR_PIXEL = divmod(INTERSECTION, PATCH)
LANES = 256
VMEM = 56 * 2**20

norm_eps = 1e-06
bf16 = jnp.bfloat16
f32 = jnp.float32

NN = (((1,), (0,)), ((), ()))
NT = (((1,), (1,)), ((), ()))
TN = (((0,), (0,)), ((), ()))


def mm(left, right, dims=NN):
    return lax.dot_general(left, right, dims, preferred_element_type=f32)


def layer_norm(values, gain_row):
    average = jnp.mean(values, axis=-1, keepdims=True)
    centered = values - average
    spread = jnp.mean(centered * centered, axis=-1, keepdims=True)
    return centered * lax.rsqrt(spread + norm_eps) * gain_row


def qkv_kernel(query_blocks, scale, x_ref, loc_ref, gain_ref, w_ref, o_ref, normed_ref):
    step = pl.program_id(0)
    rows = min(128, x_ref.shape[0])

    @pl.when(step == 0)
    def _():
        def body(t, carry):
            s = pl.ds(pl.multiple_of(t * rows, rows), rows)
            residual = x_ref[s, :].astype(f32) + loc_ref[...]
            normed_ref[s, :] = layer_norm(residual, gain_ref[...].astype(f32)).astype(bf16)
            return carry

        lax.fori_loop(0, x_ref.shape[0] // rows, body, 0)

    packed = mm(w_ref[...], normed_ref[...], NT)
    o_ref[...] = (packed * jnp.where(step < query_blocks, scale, 1.0)).astype(bf16)


def project(x, location, gain, w_t):
    tokens, width = x.shape
    block = width // 2
    scale = math.log2(math.e) / math.sqrt(width // HEADS)
    return pl.pallas_call(
        functools.partial(qkv_kernel, width // block, scale),
        grid=(w_t.shape[0] // block,),
        in_specs=[
            pl.BlockSpec((tokens, width), lambda i: (0, 0)),
            pl.BlockSpec((1, width), lambda i: (0, 0)),
            pl.BlockSpec((1, width), lambda i: (0, 0)),
            pl.BlockSpec((block, width), lambda i: (i, 0)),
        ],
        out_specs=pl.BlockSpec((block, tokens), lambda i: (i, 0)),
        out_shape=jax.ShapeDtypeStruct((w_t.shape[0], tokens), bf16),
        scratch_shapes=[pltpu.VMEM((tokens, width), bf16)],
        compiler_params=pltpu.CompilerParams(vmem_limit_bytes=VMEM),
        name="project",
    )(x, location, gain, w_t)


def attention_kernel(block, q_ref, k_ref, v_ref, o_ref):
    head_width, tokens = q_ref.shape
    keys = k_ref[...]
    values = jnp.concatenate([v_ref[...], jnp.ones((16, tokens), bf16)], axis=0)
    for first in range(0, tokens, block):
        scores = mm(keys, q_ref[:, first : first + block], TN)
        highest = jnp.max(scores, axis=0, keepdims=True)
        lifted = jnp.exp2(scores - highest).astype(bf16)
        mixed = mm(values, lifted)
        o_ref[:, first : first + block] = (
            mixed[:head_width] * (1.0 / mixed[head_width : head_width + 1])
        ).astype(bf16)


def attend(packed):
    width, tokens = packed.shape[0] // 3, packed.shape[1]
    head = width // HEADS
    return pl.pallas_call(
        functools.partial(attention_kernel, min(512, tokens)),
        grid=(HEADS,),
        in_specs=[
            pl.BlockSpec((head, tokens), lambda h: (h, 0)),
            pl.BlockSpec((head, tokens), lambda h: (h + HEADS, 0)),
            pl.BlockSpec((head, tokens), lambda h: (h + 2 * HEADS, 0)),
        ],
        out_specs=pl.BlockSpec((head, tokens), lambda h: (h, 0)),
        out_shape=jax.ShapeDtypeStruct((width, tokens), bf16),
        compiler_params=pltpu.CompilerParams(vmem_limit_bytes=VMEM),
        name="attend",
    )(packed, packed, packed)


def reduce_kernel(m_ref, w_ref, x_ref, loc_ref, gain_ref, wr_ref, bias_ref, o_ref, sum_ref):
    date = pl.program_id(0)
    updated = x_ref[...].astype(f32) + loc_ref[...] + mm(m_ref[...], w_ref[...], TN)
    encoded = layer_norm(updated, gain_ref[...].astype(f32)).astype(bf16)
    part = mm(encoded, wr_ref[...])

    @pl.when(date == 0)
    def _():
        sum_ref[...] = part

    @pl.when(date > 0)
    def _():
        sum_ref[...] += part

    @pl.when(date == pl.num_programs(0) - 1)
    def _():
        v = sum_ref[...] + bias_ref[...].astype(f32)
        o_ref[...] = (0.5 * v * (1.0 + lax.erf(v * math.sqrt(0.5)))).astype(bf16)


def reduce_dates(mixed, out_weight, x, location, gain, reduce_weight, reduce_bias):
    width, tokens = mixed.shape
    patches = tokens // DATES
    dec = reduce_weight.shape[1]
    return pl.pallas_call(
        reduce_kernel,
        grid=(DATES,),
        in_specs=[
            pl.BlockSpec((width, patches), lambda t: (0, t)),
            pl.BlockSpec((width, width), lambda t: (0, 0)),
            pl.BlockSpec((patches, width), lambda t: (t, 0)),
            pl.BlockSpec((1, width), lambda t: (0, 0)),
            pl.BlockSpec((1, width), lambda t: (0, 0)),
            pl.BlockSpec((width, dec), lambda t: (t, 0)),
            pl.BlockSpec((1, dec), lambda t: (0, 0)),
        ],
        out_specs=pl.BlockSpec((patches, dec), lambda t: (0, 0)),
        out_shape=jax.ShapeDtypeStruct((patches, dec), bf16),
        scratch_shapes=[pltpu.VMEM((patches, dec), f32)],
        compiler_params=pltpu.CompilerParams(vmem_limit_bytes=VMEM),
        name="reduce_dates",
    )(mixed, out_weight, x, location, gain, reduce_weight, reduce_bias)


FIRST_OWN = RIM // PATCH
LAST_OWN = PATCHES - 1 - FIRST_OWN
UPPER = [a for a in range(PATCHES) if PATCH * a + PATCH >= TILE_PX - RIM]
LOWER = [a for a in range(PATCHES) if PATCH * a - 1 < RIM]
ENTRIES = (
    [(0, a) for a in UPPER]
    + [(0, None)]
    + [(1, a) for a in range(FIRST_OWN, LAST_OWN + 1)]
    + [(2, a) for a in LOWER]
    + [(2, None)]
)
SIDE = 16


def decoder_kernels(upsample_weight, class_weight):
    channels = upsample_weight.shape[0]
    classes = class_weight.shape[1]
    taps = class_weight.reshape(3, 3, classes, FEAT)
    reach = np.zeros((3, PATCH, SPAN), np.float32)
    for dy in range(3):
        for i in range(PATCH):
            reach[dy, i, i + 2 - dy] = 1.0
    main = jnp.einsum("yxkf,yiI->xfikI", taps, jnp.asarray(reach, bf16), preferred_element_type=f32)
    main = main.reshape(3, FEAT, PATCH, classes * SPAN)
    far = np.arange(PATCH)[None, None, :, None] == FAR_PIXEL
    near = np.arange(PATCH)[None, None, :, None] == NEAR_PIXEL
    above = jnp.where(far, taps[0].transpose(0, 2, 1)[:, :, None, :], 0).astype(f32)
    below = jnp.where(near, taps[2].transpose(0, 2, 1)[:, :, None, :], 0).astype(f32)
    spare = jnp.zeros((3, FEAT, PATCH, LANES - classes * (SPAN + 2)), f32)
    spread = jnp.concatenate([main, above, below, spare], axis=-1).astype(bf16)
    spread = spread.reshape(3, FEAT * PATCH, LANES)
    columns = upsample_weight.reshape(channels, FEAT * PATCH, PATCH).transpose(2, 0, 1)
    columns = jnp.pad(columns, ((2, 2), (0, 0), (0, 0)))

    def kernel(first_ref, second_ref, third_ref, spread_ref, o_ref):
        total = mm(first_ref[0], spread_ref[0])
        total += mm(second_ref[0], spread_ref[1])
        total += mm(third_ref[0], spread_ref[2])
        o_ref[0] = total.astype(bf16)

    block = (1, channels, FEAT * PATCH)
    kernels = pl.pallas_call(
        kernel,
        grid=(SPAN,),
        in_specs=[
            pl.BlockSpec(block, lambda j: (j, 0, 0)),
            pl.BlockSpec(block, lambda j: (j + 1, 0, 0)),
            pl.BlockSpec(block, lambda j: (j + 2, 0, 0)),
            pl.BlockSpec((3, FEAT * PATCH, LANES), lambda j: (0, 0, 0)),
        ],
        out_specs=pl.BlockSpec((1, channels, LANES), lambda j: (j, 0, 0)),
        out_shape=jax.ShapeDtypeStruct((SPAN, channels, LANES), bf16),
        name="decoder_kernels",
    )(columns, columns, columns, spread)
    near_column = mm(columns[NEAR_PIXEL + 2], spread[2]).astype(bf16)
    far_column = mm(columns[FAR_PIXEL + 2], spread[0]).astype(bf16)
    return kernels, jnp.stack([near_column, far_column])


def neighbour_profiles(blend_weights, tile_valid):
    profiles = blend_weights.reshape(2, TILE_PX).astype(bf16)
    valid = tile_valid.reshape(1).astype(bf16)
    own = jnp.concatenate([profiles[:1] * valid, profiles[1:]], axis=0)
    before, after = neighbours((own, own), "col", lax.axis_size("col"))
    wide = jnp.stack([before, own, after])
    rows = lax.axis_size("date") * lax.axis_size("tile")
    above, below = neighbours((wide, wide), ("date", "tile"), rows)
    return jnp.stack([above, wide, below])


def rim_profile(profiles, position):
    blank = jnp.zeros(profiles.shape[:-1] + (STRIDE - RIM,), profiles.dtype)
    if position == 0:
        return jnp.concatenate([profiles[..., TILE_PX - RIM :], blank], axis=-1)
    if position == 2:
        return jnp.concatenate([blank, profiles[..., :RIM]], axis=-1)
    return profiles[..., RIM : RIM + STRIDE]


def placement():
    main = np.zeros((3, SPAN, PATCHES, STRIDE), np.float32)
    side = np.zeros((3, SIDE, STRIDE), np.float32)
    for j in range(SPAN):
        for slot in range(PATCHES):
            if slot == 0:
                which, x = 0, PATCH * (PATCHES - 1) + j - 1
            elif slot == PATCHES - 1:
                which, x = 2, j - 1
            else:
                which, x = 1, PATCH * slot + j - 1
            column = x + (0, 1, 2)[which] * STRIDE - STRIDE - RIM
            if 0 <= x < TILE_PX and 0 <= column < STRIDE:
                main[which, j, slot, column] = 1.0
    rows = []
    for j in range(SPAN):
        x = PATCH * (PATCHES - 2) + j - 1
        if TILE_PX - RIM <= x < TILE_PX:
            side[0, len(rows), x - (TILE_PX - RIM)] = 1.0
            rows.append((0, j))
    for j in range(SPAN):
        x = PATCH + j - 1
        if 0 <= x < RIM:
            side[2, len(rows), STRIDE - RIM + x] = 1.0
            rows.append((2, j))
    side[0, len(rows), RIM - 1] = 1.0
    side[2, len(rows) + 1, STRIDE - RIM] = 1.0
    return main.reshape(3, SPAN * PATCHES, STRIDE), side, rows


PLACE_MAIN, PLACE_SIDE, SIDE_ROWS = placement()


def entry_weights(row_profiles, classes):
    padded = jnp.pad(row_profiles, ((0, 0), (0, 0), (1, 1)))
    lines = []
    for tile_row, a in ENTRIES:
        if a is None:
            lines.append(jnp.zeros((3, SPAN), f32))
        else:
            lines.append(padded[tile_row, :, PATCH * a : PATCH * a + SPAN])
    lines = jnp.stack(lines)
    main = jnp.broadcast_to(lines[:, :, None, :], (len(ENTRIES), 3, classes, SPAN))
    main = main.reshape(len(ENTRIES), 3, classes * SPAN)
    halo = []
    for tile_row, a in ENTRIES:
        above = row_profiles[tile_row, :, :1] if a is None and tile_row == 2 else jnp.zeros((3, 1), f32)
        below = row_profiles[tile_row, :, -1:] if a is None and tile_row == 0 else jnp.zeros((3, 1), f32)
        halo.append(
            jnp.concatenate(
                [
                    jnp.broadcast_to(above, (3, classes)),
                    jnp.broadcast_to(below, (3, classes)),
                    jnp.zeros((3, LANES - classes * (SPAN + 2)), f32),
                ],
                axis=-1,
            )
        )
    return jnp.concatenate([main, jnp.stack(halo)], axis=-1)


def blend_tables(profiles, classes):
    row_profiles, col_profiles = profiles[:, :, 0], profiles[:, :, 1]
    weights = entry_weights(row_profiles, classes)
    before, own, after = (weights[:, i : i + 1].astype(bf16) for i in range(3))
    count = len(ENTRIES)
    main = jnp.concatenate([before, jnp.broadcast_to(own, (count, PATCHES - 2, LANES)), after], axis=1)
    side_parts = [before if which == 0 else after for which, _ in SIDE_ROWS] + [before, after]
    side_parts.append(jnp.zeros((count, SIDE - len(side_parts), LANES), bf16))
    side = jnp.concatenate(side_parts, axis=1)
    columns = jnp.stack([rim_profile(col_profiles[:, i], i) for i in range(3)], axis=1)
    rows = jnp.stack([rim_profile(row_profiles[i], i) for i in range(3)], axis=0)
    spots = sum(PLACE_MAIN[i][None] * columns[:, i, None, :] for i in range(3)).astype(bf16)
    side_spots = sum(PLACE_SIDE[i][None] * columns[:, i, None, :] for i in range(3)).astype(bf16)
    total = 0.0
    for i in range(3):
        for j in range(3):
            total = total + rows[i, j, :, None] * columns[i, j, None, :]
    return main.reshape(-1, LANES), side.reshape(-1, LANES), spots, side_spots, total


def compose_kernel(
    classes, a_ref, b_ref, rwa_ref, rwb_ref, m_ref, edge_ref, e_ref, e2_ref, den_ref, bias_ref, o_ref, z_ref, z2_ref, acc_ref
):
    count = len(ENTRIES)

    def column(j, carry):
        z = mm(a_ref[...], m_ref[j]) * rwa_ref[...].astype(f32)
        z_ref[:, j] = z.astype(bf16).reshape(count, PATCHES, LANES)
        return carry

    lax.fori_loop(0, SPAN, column, 0)
    slot = lax.broadcasted_iota(jnp.int32, b_ref.shape, 0) % SIDE
    b = b_ref[...].astype(f32)
    total = None
    for i in range(len(SIDE_ROWS) + 2):
        weights = m_ref[SIDE_ROWS[i][1]] if i < len(SIDE_ROWS) else edge_ref[i - len(SIDE_ROWS)]
        part = mm(jnp.where(slot == i, b, 0.0).astype(bf16), weights)
        total = part if total is None else total + part
    z2_ref[...] = (total * rwb_ref[...].astype(f32)).astype(bf16).reshape(count, SIDE, LANES)
    acc_ref[...] = jnp.zeros_like(acc_ref)
    for n, (tile_row, a) in enumerate(ENTRIES):
        part = mm(z_ref[n].reshape(SPAN * PATCHES, LANES), e_ref[tile_row], TN)
        part += mm(z2_ref[n], e2_ref[tile_row], TN)
        if a is None:
            first = classes * SPAN + (classes if tile_row == 0 else 0)
            y = 2 * RIM - 1 if tile_row == 0 else STRIDE
            for k in range(classes):
                acc_ref[k, y : y + 1, :] += part[first + k : first + k + 1]
            continue
        y = PATCH * a - 1 + (tile_row - 1) * STRIDE
        low, high = 0, SPAN
        if tile_row == 0:
            high = min(SPAN, TILE_PX - (PATCH * a - 1))
        if tile_row == 2:
            low = max(0, 1 - PATCH * a)
        for k in range(classes):
            acc_ref[k, y + low : y + high, :] += part[k * SPAN + low : k * SPAN + high]
    den = den_ref[...]
    inverse = 1.0 / jnp.maximum(den, 1.0)
    for k in range(classes):
        o_ref[k] = (acc_ref[k, RIM : RIM + STRIDE, :] + bias_ref[k] * den) * inverse


def neighbours(value, axis, size):
    forward = [(i, i + 1) for i in range(size - 1)]
    backward = [(i + 1, i) for i in range(size - 1)]
    return lax.ppermute(value[0], axis, forward), lax.ppermute(value[1], axis, backward)


def compose(reduced, kernels, edges, tables, class_bias, classes):
    channels = reduced.shape[1]
    own = reduced.reshape(PATCHES, PATCHES, channels)
    edge = len(UPPER)
    before, after = neighbours((own[:, -2:], own[:, :2]), "col", lax.axis_size("col"))
    wide = jnp.concatenate([own, before, after], axis=1)
    rows = lax.axis_size("date") * lax.axis_size("tile")
    above, below = neighbours((wide[-edge:], wide[: len(LOWER)]), ("date", "tile"), rows)
    lines = jnp.concatenate(
        [
            above,
            wide[NEAR_PATCH : NEAR_PATCH + 1],
            wide[FIRST_OWN : LAST_OWN + 1],
            below,
            wide[FAR_PATCH : FAR_PATCH + 1],
        ],
        axis=0,
    )
    count = len(ENTRIES)
    main = jnp.concatenate([lines[:, PATCHES + 1 : PATCHES + 2], lines[:, 1 : PATCHES - 1], lines[:, PATCHES + 2 : PATCHES + 3]], axis=1)
    parts = [lines[:, PATCHES : PATCHES + 1] if which == 0 else lines[:, PATCHES + 3 : PATCHES + 4] for which, _ in SIDE_ROWS]
    parts += [lines[:, NEAR_PATCH : NEAR_PATCH + 1], lines[:, FAR_PATCH : FAR_PATCH + 1]]
    parts.append(jnp.zeros((count, SIDE - len(parts), channels), bf16))
    side = jnp.concatenate(parts, axis=1)
    main_weights, side_weights, spots, side_spots, total = tables
    whole = pl.BlockSpec(memory_space=pltpu.VMEM)
    return pl.pallas_call(
        functools.partial(compose_kernel, classes),
        in_specs=[whole] * 9 + [pl.BlockSpec(memory_space=pltpu.SMEM)],
        out_specs=whole,
        out_shape=jax.ShapeDtypeStruct((classes, STRIDE, STRIDE), f32),
        scratch_shapes=[
            pltpu.VMEM((count, SPAN, PATCHES, LANES), bf16),
            pltpu.VMEM((count, SIDE, LANES), bf16),
            pltpu.VMEM((classes, TILE_PX, STRIDE), f32),
        ],
        compiler_params=pltpu.CompilerParams(vmem_limit_bytes=VMEM),
        name="compose",
    )(
        main.reshape(-1, channels),
        side.reshape(-1, channels),
        main_weights,
        side_weights,
        kernels,
        edges,
        spots,
        side_spots,
        total,
        class_bias.astype(f32),
    )


def local(
    arrivals,
    owner_map,
    block_ids,
    tile_valid,
    blend_weights,
    location_table,
    norm_gain,
    qkv_weight,
    out_weight,
    final_gain,
    reduce_weight,
    reduce_bias,
    upsample_weight,
    class_weight,
    class_bias,
):
    width = arrivals.shape[-1]
    classes = class_weight.shape[1]
    profiles = neighbour_profiles(blend_weights, tile_valid).astype(f32)
    order = jnp.argsort(owner_map[0])
    ordered = jnp.take(arrivals[0], order, axis=0, mode="clip")
    strip = ordered.shape[3] * ordered.shape[4]
    ordered = ordered.reshape(ordered.shape[0], strip, width)
    ordered, profiles, qkv_weight, upsample_weight, class_weight = lax.optimization_barrier(
        (ordered, profiles, qkv_weight, upsample_weight, class_weight)
    )
    x = lax.all_to_all(ordered, ("date", "tile"), split_axis=0, concat_axis=0, tiled=True)
    codes = block_ids.reshape(1, 1)
    one_hot = (codes == jnp.arange(location_table.shape[0], dtype=jnp.int32)[None, :]).astype(bf16)
    location = jnp.dot(one_hot, location_table, preferred_element_type=f32)

    qkv_t = qkv_weight.T
    kernels, edges = decoder_kernels(upsample_weight, class_weight)
    tables = blend_tables(profiles, classes)
    x, location, qkv_t, kernels, edges, tables = lax.optimization_barrier((x, location, qkv_t, kernels, edges, tables))
    x = x.reshape(-1, width)

    packed = project(x, location, norm_gain[None], qkv_t)
    mixed = attend(packed)
    reduced = reduce_dates(mixed, out_weight, x, location, final_gain[None], reduce_weight, reduce_bias[None])
    return compose(reduced, kernels, edges, tables, class_bias, classes)[None]


def solution(mesh):
    placed = (
        P(None, None, "col", "date", "tile", None, None),
        P(),
        P(None, ("date", "tile"), "col"),
        P(None, ("date", "tile"), "col"),
        P(None, ("date", "tile"), "col", None, None),
    ) + (P(),) * 10
    return jax.shard_map(
        local,
        mesh=mesh,
        in_specs=placed,
        out_specs=P(None, None, ("date", "tile"), "col"),
        check_vma=False,
    )
```

```python
import functools
import math

import jax
import jax.numpy as jnp
import numpy as np
from jax import lax
from jax.experimental import pallas as pl
from jax.experimental.pallas import tpu as pltpu
from jax.sharding import PartitionSpec as P

HEADS = 16
DATES = 4
PATCH = 14
INTERSECTION = 32
FEAT = 16
PATCHES = 16
RIM = 16
TILE_PX = PATCH * PATCHES
STRIDE = TILE_PX - INTERSECTION
SPAN = PATCH + 2
FAR_PATCH, FAR_PIXEL = divmod(STRIDE - 1, PATCH)
NEAR_PATCH, NEAR_PIXEL = divmod(INTERSECTION, PATCH)
LANES = 256
VMEM = 56 * 2**20

EXPONENT_BOUND = 100.0
SUM_ROWS = 16
PAIR = 2
GROUP = 256

norm_eps = 1e-06
bf16 = jnp.bfloat16
f32 = jnp.float32

NN = (((1,), (0,)), ((), ()))
NT = (((1,), (1,)), ((), ()))
TN = (((0,), (0,)), ((), ()))


def mm(left, right, dims=NN):
    return lax.dot_general(left, right, dims, preferred_element_type=f32)


def layer_norm(values, gain_row):
    average = jnp.mean(values, axis=-1, keepdims=True)
    centered = values - average
    spread = jnp.mean(centered * centered, axis=-1, keepdims=True)
    return centered * lax.rsqrt(spread + norm_eps) * gain_row


def gather_kernel(routes, index_ref, a_ref, *refs):
    outs, (held, in_sems, out_sems) = refs[:-3], refs[-3:]
    loads = [pltpu.make_async_copy(a_ref.at[index_ref[n]], held.at[n], in_sems.at[n]) for n in range(len(routes))]
    for load in loads:
        load.start()
    stores = []
    for n, (out, spot) in enumerate(routes):
        loads[n].wait()
        stores.append(pltpu.make_async_copy(held.at[n], outs[out].at[spot], out_sems.at[n]))
        stores[n].start()
    for store in stores:
        store.wait()


def gather_pieces(arrivals, owner_map, early, late, dates):
    slots, strip, width = arrivals.shape
    tiles = slots // dates
    date, tile = lax.axis_index("date"), lax.axis_index("tile")
    together = [0] + late
    routes, order = [], []
    for s in range(tiles):
        for m in range(dates):
            order.append((s, m))
            routes.append((early.index(s) - 1, m) if s in early[1:] else (len(early) - 1 + m, together.index(s)))
    s_of = jnp.array([s for s, _ in order], jnp.int32)
    m_of = jnp.array([m for _, m in order], jnp.int32)
    wanted = (date ^ m_of) * tiles + (tile ^ s_of)
    spots = jnp.arange(slots, dtype=jnp.int32)[None, :]
    index = jnp.sum(jnp.where(owner_map[None, :] == wanted[:, None], spots, 0), axis=1)
    shapes = [jax.ShapeDtypeStruct((dates, strip, width), bf16)] * (len(early) - 1)
    shapes += [jax.ShapeDtypeStruct((len(together), strip, width), bf16)] * dates
    anywhere = pl.BlockSpec(memory_space=pl.ANY)
    outs = pl.pallas_call(
        functools.partial(gather_kernel, routes),
        in_specs=[pl.BlockSpec(memory_space=pltpu.SMEM), anywhere],
        out_specs=[anywhere] * len(shapes),
        out_shape=shapes,
        scratch_shapes=[
            pltpu.VMEM(arrivals.shape, bf16),
            pltpu.SemaphoreType.DMA((slots,)),
            pltpu.SemaphoreType.DMA((slots,)),
        ],
        compiler_params=pltpu.CompilerParams(vmem_limit_bytes=16 * 2**20),
        name="gather_pieces",
    )(index, arrivals)
    return outs[: len(early) - 1], outs[len(early) - 1 :]


def swap(value, axis, mask):
    return lax.ppermute(value, axis, [(i, i ^ mask) for i in range(lax.axis_size(axis))])


def exchange(arrivals, owner_map):
    dates, tiles = lax.axis_size("date"), lax.axis_size("tile")
    late = list(range(tiles - max(1, tiles // 4), tiles))
    early = list(range(tiles - len(late)))
    rings, mixed = gather_pieces(arrivals, owner_map, early, late, dates)
    rings = [swap(ring, "tile", s) for s, ring in zip(early[1:], rings)]
    mixed = [value if m == 0 else swap(value, "date", m) for m, value in enumerate(mixed)]
    last = []
    for i, s in enumerate(late):
        pieces = jnp.stack([value[1 + i] for value in mixed])
        last.append(swap(pieces, "tile", s))
    first = [(value, 0) for value in mixed]
    for ring in rings:
        first += [(ring, 0) if m == 0 else (swap(ring[m : m + 1], "date", m), 0) for m in range(dates)]
    return first, [(value, m) for value in last for m in range(dates)]


def project_kernel(pieces, *refs):
    x_refs, (loc_ref, gain_ref, w_ref, o_ref, norm_ref, x_out, normed_ref) = refs[:pieces], refs[pieces:]
    step = pl.program_id(0)

    @pl.when(step == 0)
    def _():
        first = 0
        for x_ref in x_refs:
            for row in range(0, x_ref.shape[0], 64):
                x = x_ref[row : row + 64, :]
                x_out[first : first + x.shape[0], :] = x
                residual = x.astype(f32) + loc_ref[...]
                normed = layer_norm(residual, gain_ref[...].astype(f32))
                normed_ref[first : first + x.shape[0], :] = normed.astype(bf16)
                first += x.shape[0]

    packed = mm(w_ref[...], normed_ref[...], (((0,), (1,)), ((), ())))
    packed = packed.astype(bf16)
    o_ref[...] = packed
    packed = packed.astype(f32)
    heads = norm_ref.shape[0]
    squares = jnp.sum((packed * packed).reshape(heads, packed.shape[0] // heads, packed.shape[1]), axis=1)
    norm_ref[...] = jnp.broadcast_to(jnp.max(squares, axis=1, keepdims=True), norm_ref.shape)


def project(pieces, location, gain, weight):
    width = weight.shape[0]
    tokens = sum(piece.shape[1] for piece, _ in pieces)
    block = width // 2
    steps = weight.shape[1] // block
    row = pl.BlockSpec((1, width), lambda i: (0, 0))
    return pl.pallas_call(
        functools.partial(project_kernel, len(pieces)),
        grid=(steps,),
        in_specs=[pl.BlockSpec((None,) + piece.shape[1:], lambda i, n=n: (n, 0, 0)) for piece, n in pieces]
        + [row, row, pl.BlockSpec((width, block), lambda i: (0, i))],
        out_specs=[
            pl.BlockSpec((block, tokens), lambda i: (i, 0)),
            pl.BlockSpec((3 * HEADS // steps, 128), lambda i: (i, 0)),
            pl.BlockSpec((tokens, width), lambda i: (0, 0)),
        ],
        out_shape=[
            jax.ShapeDtypeStruct((weight.shape[1], tokens), bf16),
            jax.ShapeDtypeStruct((3 * HEADS, 128), f32),
            jax.ShapeDtypeStruct((tokens, width), bf16),
        ],
        scratch_shapes=[pltpu.VMEM((tokens, width), bf16)],
        compiler_params=pltpu.CompilerParams(vmem_limit_bytes=VMEM),
        cost_estimate=pl.CostEstimate(
            flops=2 * tokens * width * weight.shape[1], bytes_accessed=weight.size * 2, transcendentals=0
        ),
        name="project",
    )(*[piece for piece, _ in pieces], location, gain, weight)


def with_ones(values):
    return jnp.concatenate([values, jnp.ones((SUM_ROWS, values.shape[1]), bf16)], axis=0)


def attend_kernel(parts, *refs):
    q_refs, k_refs, v_refs, norm_refs = (refs[i * parts : (i + 1) * parts] for i in range(4))
    o_ref, flag_ref = refs[4 * parts :]
    head = o_ref.shape[0] // PAIR
    scale = math.log2(math.e) / math.sqrt(head)

    @pl.when(pl.program_id(0) == 0)
    def _():
        norms = norm_refs[0][...]
        for norm_ref in norm_refs[1:]:
            norms = jnp.maximum(norms, norm_ref[...])
        flag_ref[0] = jnp.max(norms[:HEADS] * norms[HEADS : 2 * HEADS])

    small = flag_ref[0] <= (EXPONENT_BOUND / scale) ** 2

    def rows(n):
        return slice(n * head, (n + 1) * head)

    def side_by_side(part_refs, n):
        return jnp.concatenate([ref[rows(n), :] for ref in part_refs], axis=1)

    def scores(n):
        return mm(side_by_side(k_refs, n), side_by_side(q_refs, n), TN)

    def finish(n, lifted):
        sums = mm(with_ones(side_by_side(v_refs, n)), lifted.astype(bf16))
        o_ref[rows(n), :] = (sums[:head] * (1.0 / sums[head : head + 1])).astype(bf16)

    @pl.when(small)
    def _():
        for n in range(PAIR):
            finish(n, jnp.exp2(scores(n) * scale))

    @pl.when(jnp.logical_not(small))
    def _():
        for n in range(PAIR):
            held = scores(n)
            finish(n, jnp.exp2((held - jnp.max(held, axis=0, keepdims=True)) * scale))


def attend(packed, norms):
    head = packed[0].shape[0] // (3 * HEADS)
    tokens = sum(part.shape[1] for part in packed)
    steps = HEADS // PAIR
    specs = []
    for p in range(3):
        for part in packed:
            specs.append(pl.BlockSpec((PAIR * head, part.shape[1]), lambda h, p=p: (h + p * steps, 0)))
    specs += [pl.BlockSpec(norm.shape, lambda h: (0, 0)) for norm in norms]
    return pl.pallas_call(
        functools.partial(attend_kernel, len(packed)),
        grid=(steps,),
        in_specs=specs,
        out_specs=pl.BlockSpec((PAIR * head, tokens), lambda h: (h, 0)),
        out_shape=jax.ShapeDtypeStruct((HEADS * head, tokens), bf16),
        scratch_shapes=[pltpu.SMEM((1,), f32)],
        compiler_params=pltpu.CompilerParams(vmem_limit_bytes=VMEM),
        name="attend",
    )(*(list(packed) * 3), *norms)


def reduce_kernel(
    place_ref, m_ref, w_ref, x0_ref, x1_ref, loc_ref, gain_ref, wr_ref, bias_ref, profile_ref,
    o_ref, last_ref, first_ref, encoded_ref, reduced_ref
):
    step = pl.program_id(0)
    steps = pl.num_programs(0)
    tiles, dates, strip, width = encoded_ref.shape
    held = jnp.where(step < steps - 1, x0_ref[...].astype(f32), x1_ref[...].astype(f32))
    updated = held + loc_ref[...] + mm(m_ref[...], w_ref[...], TN)
    encoded = layer_norm(updated, gain_ref[...].astype(f32)).astype(bf16)
    part = tiles // steps
    encoded_ref[pl.ds(step * part, part)] = encoded.reshape(part, dates, strip, width)

    @pl.when(step == steps - 1)
    def _():
        total = bias_ref[...].astype(f32)
        for m in range(dates):
            total = total + mm(encoded_ref[:, m].reshape(tiles * strip, width), wr_ref[place_ref[0] ^ m])
        total = 0.5 * total * (1.0 + lax.erf(total * math.sqrt(0.5)))
        for s in range(tiles):
            spot = pl.multiple_of((place_ref[1] ^ s) * strip, strip)
            for half in range(reduced_ref.shape[0]):
                lanes = slice(128 * half, 128 * (half + 1))
                reduced_ref[half, pl.ds(spot, strip), :] = total[s * strip : (s + 1) * strip, lanes]
        for half in range(reduced_ref.shape[0]):
            o_ref[:, 128 * half : 128 * (half + 1)] = reduced_ref[half].astype(bf16)

        def column(b):
            halves = [reduced_ref[half, pl.ds(b, PATCHES, stride=PATCHES), :] for half in range(reduced_ref.shape[0])]
            return jnp.concatenate(halves, axis=1)

        tail = jnp.zeros((PATCHES - 2, o_ref.shape[1]), f32)
        tail = jnp.concatenate([profile_ref[...].astype(f32), tail], axis=0)
        last = place_ref[2] == 1
        sent = [jnp.where(last, column(PATCHES - 2 + i), column(i)) for i in range(2)]
        last_ref[...] = jnp.concatenate(sent + [tail], axis=0).astype(bf16)
        first_ref[...] = jnp.concatenate([column(0), column(1), tail], axis=0).astype(bf16)


def reduce_dates(place, mixed, out_weight, x0, x1, location, gain, reduce_weight, reduce_bias, profile, tiles, dates):
    width, tokens = mixed.shape
    strip = tokens // (tiles * dates)
    dec = reduce_weight.shape[1]
    steps = tokens // GROUP
    row = pl.BlockSpec((1, width), lambda t: (0, 0))
    sent = jax.ShapeDtypeStruct((3 * PATCHES, dec), bf16)
    sent_spec = pl.BlockSpec((3 * PATCHES, dec), lambda t: (0, 0))
    patches = tiles * strip
    return pl.pallas_call(
        reduce_kernel,
        grid=(steps,),
        in_specs=[
            pl.BlockSpec(memory_space=pltpu.SMEM),
            pl.BlockSpec((width, GROUP), lambda t: (0, t)),
            pl.BlockSpec((width, width), lambda t: (0, 0)),
            pl.BlockSpec((GROUP, width), lambda t: (jnp.minimum(t, steps - 2), 0)),
            pl.BlockSpec((GROUP, width), lambda t: (0, 0)),
            row,
            row,
            pl.BlockSpec((dates, width, dec), lambda t: (0, 0, 0)),
            pl.BlockSpec((1, dec), lambda t: (0, 0)),
            pl.BlockSpec((2, dec), lambda t: (0, 0)),
        ],
        out_specs=[pl.BlockSpec((patches, dec), lambda t: (0, 0)), sent_spec, sent_spec],
        out_shape=[jax.ShapeDtypeStruct((patches, dec), bf16), sent, sent],
        scratch_shapes=[pltpu.VMEM((tiles, dates, strip, width), bf16), pltpu.VMEM((dec // 128, patches, 128), f32)],
        compiler_params=pltpu.CompilerParams(vmem_limit_bytes=VMEM),
        name="reduce_dates",
    )(place, mixed, out_weight, x0, x1, location, gain, reduce_weight.reshape(dates, width, dec), reduce_bias, profile)


FIRST_OWN = RIM // PATCH
LAST_OWN = PATCHES - 1 - FIRST_OWN
UPPER = [a for a in range(PATCHES) if PATCH * a + PATCH >= TILE_PX - RIM]
LOWER = [a for a in range(PATCHES) if PATCH * a - 1 < RIM]
ENTRIES = (
    [(0, a) for a in UPPER]
    + [(0, None)]
    + [(1, a) for a in range(FIRST_OWN, LAST_OWN + 1)]
    + [(2, a) for a in LOWER]
    + [(2, None)]
)
SIDE = 16


def placement():
    main = np.zeros((3, SPAN, PATCHES, STRIDE), np.float32)
    side = np.zeros((3, SIDE, STRIDE), np.float32)
    for j in range(SPAN):
        for slot in range(PATCHES):
            if slot == 0:
                which, x = 0, PATCH * (PATCHES - 1) + j - 1
            elif slot == PATCHES - 1:
                which, x = 2, j - 1
            else:
                which, x = 1, PATCH * slot + j - 1
            column = x + (which - 1) * STRIDE - RIM
            if 0 <= x < TILE_PX and 0 <= column < STRIDE:
                main[which, j, slot, column] = 1.0
    rows = []
    for j in range(SPAN):
        x = PATCH * (PATCHES - 2) + j - 1
        if TILE_PX - RIM <= x < TILE_PX:
            side[0, len(rows), x - (TILE_PX - RIM)] = 1.0
            rows.append((0, j))
    for j in range(SPAN):
        x = PATCH + j - 1
        if 0 <= x < RIM:
            side[2, len(rows), STRIDE - RIM + x] = 1.0
            rows.append((2, j))
    side[0, len(rows), RIM - 1] = 1.0
    side[2, len(rows) + 1, STRIDE - RIM] = 1.0
    return main.reshape(3, SPAN * PATCHES, STRIDE), side, rows


PLACE_MAIN, PLACE_SIDE, SIDE_ROWS = placement()


def windows():
    table = np.zeros((3, LANES, STRIDE), np.float32)
    for x in range(STRIDE):
        table[1, x + RIM, x] = 1.0
    for x in range(RIM):
        table[0, TILE_PX - RIM + x, x] = 1.0
        table[2, x, STRIDE - RIM + x] = 1.0
    return table


def row_lanes(classes):
    table = np.zeros((LANES, len(ENTRIES), LANES), np.float32)
    for n, (tile_row, a) in enumerate(ENTRIES):
        for k in range(classes):
            if a is None:
                halo = classes * SPAN + k + (classes if tile_row == 0 else 0)
                table[TILE_PX - 1 if tile_row == 0 else 0, n, halo] = 1.0
                continue
            for i in range(SPAN):
                y = PATCH * a - 1 + i
                if 0 <= y < TILE_PX:
                    table[y, n, k * SPAN + i] = 1.0
    return table.reshape(LANES, -1)


def tap_tables(classes):
    rows = np.zeros((LANES, classes), np.float32)
    columns = np.zeros((FEAT, FEAT * PATCH), np.float32)
    meet = np.zeros((3, LANES, FEAT, PATCH), np.float32)
    for f in range(FEAT):
        columns[f, f * PATCH : (f + 1) * PATCH] = 1.0
    for k in range(classes):
        rows[k * SPAN : (k + 1) * SPAN, k] = 1.0
        rows[classes * SPAN + k, k] = 1.0
        rows[classes * (SPAN + 1) + k, k] = 1.0
        for dy in range(3):
            for i in range(PATCH):
                meet[dy, k * SPAN + i + 2 - dy, :, i] = 1.0
        meet[0, classes * SPAN + k, :, FAR_PIXEL] = 1.0
        meet[2, classes * (SPAN + 1) + k, :, NEAR_PIXEL] = 1.0
    return rows, columns, meet.reshape(3, LANES, FEAT * PATCH)


def kernels_kernel(up_ref, taps_ref, rows_ref, columns_ref, meet_ref, o_ref, edge_ref, turned_ref, column_ref):
    for half in range(turned_ref.shape[0]):
        lanes = slice(128 * half, 128 * (half + 1))
        turned_ref[half] = up_ref[lanes, :].astype(f32).T
        for j in range(PATCH):
            column_ref[j, :, lanes] = turned_ref[half, pl.ds(j, FEAT * PATCH, stride=PATCH), :].astype(bf16)
    spread = []
    for dx in range(3):
        total = None
        for dy in range(3):
            taps = mm(mm(rows_ref[...], taps_ref[3 * dy + dx]).astype(bf16), columns_ref[...])
            part = taps * meet_ref[dy].astype(f32)
            total = part if total is None else total + part
        spread.append(total.astype(bf16))
    for big in range(SPAN):
        total = None
        for dx in range(3):
            j = big - 2 + dx
            if 0 <= j < PATCH:
                part = mm(spread[dx], column_ref[j])
                total = part if total is None else total + part
        o_ref[big] = total.astype(bf16)
    edge_ref[0] = mm(spread[2], column_ref[NEAR_PIXEL]).astype(bf16)
    edge_ref[1] = mm(spread[0], column_ref[FAR_PIXEL]).astype(bf16)


def decoder_kernels(upsample_weight, class_weight):
    channels = upsample_weight.shape[0]
    tables = [jnp.asarray(table, bf16) for table in tap_tables(class_weight.shape[1])]
    return pl.pallas_call(
        kernels_kernel,
        out_shape=[
            jax.ShapeDtypeStruct((SPAN, LANES, channels), bf16),
            jax.ShapeDtypeStruct((2, LANES, channels), bf16),
        ],
        scratch_shapes=[
            pltpu.VMEM((channels // 128, upsample_weight.shape[1], 128), f32),
            pltpu.VMEM((PATCH, FEAT * PATCH, channels), bf16),
        ],
        compiler_params=pltpu.CompilerParams(vmem_limit_bytes=VMEM),
        name="decoder_kernels",
    )(upsample_weight, class_weight, *tables)


def compose_kernel(
    classes, own_ref, before_ref, after_ref, above_ref, below_ref, profile_ref, m_ref, edge_ref,
    lanes_ref, window_ref, place_ref, side_ref, bias_ref,
    o_ref, a_ref, b_ref, z_ref, z2_ref, acc_ref
):
    count = len(ENTRIES)
    edge = len(UPPER)
    own, before, after, above, below = (
        ref[...].astype(f32) for ref in (own_ref, before_ref, after_ref, above_ref, below_ref)
    )
    slot = lax.broadcasted_iota(jnp.int32, (PATCHES, LANES), 0)

    def line(tile_row, a):
        if tile_row == 1 or a is None:
            a = a if a is not None else (NEAR_PATCH if tile_row == 0 else FAR_PATCH)
            sides = [before[a : a + 1], before[PATCHES + a : PATCHES + a + 1]]
            sides += [after[a : a + 1], after[PATCHES + a : PATCHES + a + 1]]
            return own[PATCHES * a : PATCHES * (a + 1)], sides
        source = above if tile_row == 0 else below
        n = (UPPER if tile_row == 0 else LOWER).index(a)
        first = PATCHES * edge + 4 * n
        return source[PATCHES * n : PATCHES * (n + 1)], [source[first + i : first + i + 1] for i in range(4)]

    def slots(rows, base):
        for i, row in rows.items():
            base = jnp.where(slot == i, row, base)
        return base

    def second(before_row, after_row, near, far):
        rows = {i: before_row if which == 0 else after_row for i, (which, _) in enumerate(SIDE_ROWS)}
        rows[len(SIDE_ROWS)] = near
        rows[len(SIDE_ROWS) + 1] = far
        return slots(rows, jnp.zeros((SIDE, LANES), f32))

    profile = profile_ref[...].astype(f32)
    tail = slice(2 * PATCHES, 2 * PATCHES + 2)
    ends = slice((PATCHES + 4) * edge, (PATCHES + 4) * edge + 6)
    profiles = jnp.concatenate([above[ends], before[tail], profile, after[tail], below[ends]], axis=0)
    row_profiles = [profiles[2 * i : 2 * i + 1] for i in range(9)]
    col_profiles = [profiles[2 * i + 1 : 2 * i + 2] for i in range(9)]
    blank = jnp.zeros((PATCHES - 9, LANES), f32)
    row_table = jnp.concatenate(row_profiles + [blank], axis=0).astype(bf16)
    col_table = jnp.concatenate(col_profiles + [blank], axis=0).astype(bf16)
    weights = mm(row_table, lanes_ref[...])
    rows = [mm(row_table, window_ref[i]) for i in range(3)]
    cols = [mm(col_table, window_ref[i]) for i in range(3)]
    block_rows = jnp.concatenate([rows[i // 3][i : i + 1] for i in range(9)] + [blank[:, :STRIDE]], axis=0)
    block_cols = jnp.concatenate([cols[i % 3][i : i + 1] for i in range(9)] + [blank[:, :STRIDE]], axis=0)
    den = mm(block_rows.astype(bf16), block_cols.astype(bf16), TN)
    spots, side_spots = [], []
    for tile_row in range(3):
        spots.append(sum(place_ref[i].astype(f32) * block_cols[3 * tile_row + i][None] for i in range(3)).astype(bf16))
        side_spots.append(
            sum(side_ref[i].astype(f32) * block_cols[3 * tile_row + i][None] for i in range(3)).astype(bf16)
        )

    def entry_weights(n, tile_row):
        return [weights[3 * tile_row + i : 3 * tile_row + i + 1, LANES * n : LANES * (n + 1)] for i in range(3)]

    main_weights, side_weights = [], []
    for n, (tile_row, a) in enumerate(ENTRIES):
        patches, (l_far, l_near, r_near, r_far) = line(tile_row, a)
        a_ref[n] = slots({0: l_near, PATCHES - 1: r_near}, patches).astype(bf16)
        b_ref[n] = second(
            l_far, r_far, patches[NEAR_PATCH : NEAR_PATCH + 1], patches[FAR_PATCH : FAR_PATCH + 1]
        ).astype(bf16)
        left, middle, right = entry_weights(n, tile_row)
        main_weights.append(slots({0: left, PATCHES - 1: right}, jnp.broadcast_to(middle, (PATCHES, LANES))))
        side_weights.append(second(left, right, left, right))
    main_weights = jnp.stack(main_weights)
    for j in range(SPAN):
        z = mm(a_ref[...].reshape(count * PATCHES, LANES), m_ref[j], NT).reshape(count, PATCHES, LANES)
        z_ref[:, j] = (z * main_weights).astype(bf16)
    side_slot = lax.broadcasted_iota(jnp.int32, (count, SIDE, LANES), 1)
    patches = b_ref[...].astype(f32)
    total = None
    for i in range(len(SIDE_ROWS) + 2):
        kernel = m_ref[SIDE_ROWS[i][1]] if i < len(SIDE_ROWS) else edge_ref[i - len(SIDE_ROWS)]
        part = jnp.where(side_slot == i, patches, 0.0).astype(bf16).reshape(count * SIDE, LANES)
        part = mm(part, kernel, NT)
        total = part if total is None else total + part
    z2_ref[...] = (total.reshape(count, SIDE, LANES) * jnp.stack(side_weights)).astype(bf16)

    acc_ref[...] = jnp.zeros_like(acc_ref)
    for n, (tile_row, a) in enumerate(ENTRIES):
        part = mm(z_ref[n].reshape(SPAN * PATCHES, LANES), spots[tile_row], TN)
        part += mm(z2_ref[n], side_spots[tile_row], TN)
        if a is None:
            first = classes * SPAN + (classes if tile_row == 0 else 0)
            y = 2 * RIM - 1 if tile_row == 0 else STRIDE
            for k in range(classes):
                acc_ref[k, y : y + 1, :] += part[first + k : first + k + 1]
            continue
        y = PATCH * a - 1 + (tile_row - 1) * STRIDE
        low, high = 0, SPAN
        if tile_row == 0:
            high = min(SPAN, TILE_PX - (PATCH * a - 1))
        if tile_row == 2:
            low = max(0, 1 - PATCH * a)
        for k in range(classes):
            acc_ref[k, y + low : y + high, :] += part[k * SPAN + low : k * SPAN + high]
    inverse = 1.0 / jnp.maximum(den, 1.0)
    for k in range(classes):
        o_ref[k] = (acc_ref[k, RIM : RIM + STRIDE, :] + bias_ref[k] * den) * inverse


def forward(size):
    return [(i, i + 1) for i in range(size - 1)]


def backward(size):
    return [(i + 1, i) for i in range(size - 1)]


def exchange_rims(reduced, last, first, profile):
    cols = lax.axis_size("col")
    if cols == 2:
        other = swap(last, "col", 1)
        at_end = lax.axis_index("col") == 1
        before, after = jnp.where(at_end, other, 0), jnp.where(at_end, 0, other)
    else:
        before = lax.ppermute(last, "col", forward(cols))
        after = lax.ppermute(first, "col", backward(cols))

    def lines(rows):
        parts = [reduced[PATCHES * a : PATCHES * (a + 1)] for a in rows]
        for a in rows:
            for side in (before, after):
                parts += [side[a : a + 1], side[PATCHES + a : PATCHES + a + 1]]
        parts += [before[2 * PATCHES : 2 * PATCHES + 2], profile, after[2 * PATCHES : 2 * PATCHES + 2]]
        used = (PATCHES + 4) * len(rows) + 6
        parts.append(jnp.zeros((-used % 16, reduced.shape[1]), bf16))
        return jnp.concatenate(parts, axis=0)

    rows = lax.axis_size("date") * lax.axis_size("tile")
    above = lax.ppermute(lines(UPPER), ("date", "tile"), forward(rows))
    below = lax.ppermute(lines(LOWER), ("date", "tile"), backward(rows))
    return before, after, above, below


def compose(reduced, rims, profile, kernels, edges, class_bias, classes):
    channels = reduced.shape[1]
    count = len(ENTRIES)
    whole = pl.BlockSpec(memory_space=pltpu.VMEM)
    tables = [jnp.asarray(t, bf16) for t in (row_lanes(classes), windows(), PLACE_MAIN, PLACE_SIDE)]
    return pl.pallas_call(
        functools.partial(compose_kernel, classes),
        in_specs=[whole] * 12 + [pl.BlockSpec(memory_space=pltpu.SMEM)],
        out_specs=whole,
        out_shape=jax.ShapeDtypeStruct((classes, STRIDE, STRIDE), f32),
        scratch_shapes=[
            pltpu.VMEM((count, PATCHES, channels), bf16),
            pltpu.VMEM((count, SIDE, channels), bf16),
            pltpu.VMEM((count, SPAN, PATCHES, LANES), bf16),
            pltpu.VMEM((count, SIDE, LANES), bf16),
            pltpu.VMEM((classes, TILE_PX, STRIDE), f32),
        ],
        compiler_params=pltpu.CompilerParams(vmem_limit_bytes=VMEM),
        name="compose",
    )(reduced, *rims, profile, kernels, edges, *tables, class_bias.astype(f32))


def local(
    arrivals,
    owner_map,
    block_ids,
    tile_valid,
    blend_weights,
    location_table,
    norm_gain,
    qkv_weight,
    out_weight,
    final_gain,
    reduce_weight,
    reduce_bias,
    upsample_weight,
    class_weight,
    class_bias,
):
    width = arrivals.shape[-1]
    slots = arrivals.shape[1]
    classes = class_weight.shape[1]
    dates, tiles = lax.axis_size("date"), lax.axis_size("tile")
    first, last = exchange(arrivals.reshape(slots, -1, width), owner_map[0])

    codes = block_ids.reshape(1, 1)
    one_hot = (codes == jnp.arange(location_table.shape[0], dtype=jnp.int32)[None, :]).astype(bf16)
    location = jnp.dot(one_hot, location_table, preferred_element_type=f32)
    profile = blend_weights.reshape(2, TILE_PX).astype(bf16)
    profile = jnp.concatenate([profile[:1] * tile_valid.reshape(1).astype(bf16), profile[1:]], axis=0)
    profile = jnp.pad(profile, ((0, 0), (0, LANES - TILE_PX)))
    kernels, edges = decoder_kernels(upsample_weight, class_weight)

    arrays = [array for array, _ in first]
    arrays, location, profile, kernels, edges = lax.optimization_barrier((arrays, location, profile, kernels, edges))
    first = [(array, n) for array, (_, n) in zip(arrays, first)]
    packed0, norms0, x0 = project(first, location, norm_gain[None], qkv_weight)
    packed1, norms1, x1 = project(last, location, norm_gain[None], qkv_weight)
    mixed = attend([packed0, packed1], [norms0, norms1])
    go_last = jnp.where((lax.axis_index("col") == 0) | (lax.axis_size("col") != 2), 1, 0)
    place = jnp.stack([lax.axis_index("date"), lax.axis_index("tile"), go_last]).astype(jnp.int32)
    reduced, to_after, to_before = reduce_dates(
        place, mixed, out_weight, x0, x1, location, final_gain[None], reduce_weight, reduce_bias[None], profile, tiles, dates
    )
    rims = exchange_rims(reduced, to_after, to_before, profile)
    return compose(reduced, rims, profile, kernels, edges, class_bias, classes)[None]


def solution(mesh):
    placed = (
        P(None, None, "col", "date", "tile", None, None),
        P(),
        P(None, ("date", "tile"), "col"),
        P(None, ("date", "tile"), "col"),
        P(None, ("date", "tile"), "col", None, None),
    ) + (P(),) * 10
    return jax.shard_map(
        local,
        mesh=mesh,
        in_specs=placed,
        out_specs=P(None, None, ("date", "tile"), "col"),
        check_vma=False,
    )
```

```python
import functools
import math

import jax
import jax.numpy as jnp
import numpy as np
from jax import lax
from jax.experimental import pallas as pl
from jax.experimental.pallas import tpu as pltpu
from jax.sharding import PartitionSpec as P

HEADS = 16
DATES = 4
PATCH = 14
INTERSECTION = 32
FEAT = 16
PATCHES = 16
RIM = 16
TILE_PX = PATCH * PATCHES
STRIDE = TILE_PX - INTERSECTION
SPAN = PATCH + 2
FAR_PATCH, FAR_PIXEL = divmod(STRIDE - 1, PATCH)
NEAR_PATCH, NEAR_PIXEL = divmod(INTERSECTION, PATCH)
LANES = 256
VMEM = 56 * 2**20

EXPONENT_BOUND = 100.0
SUM_ROWS = 16
PAIR = 2
GROUP = 256

norm_eps = 1e-06
bf16 = jnp.bfloat16
f32 = jnp.float32

NN = (((1,), (0,)), ((), ()))
NT = (((1,), (1,)), ((), ()))
TN = (((0,), (0,)), ((), ()))


def mm(left, right, dims=NN):
    return lax.dot_general(left, right, dims, preferred_element_type=f32)


def layer_norm(values, gain_row):
    average = jnp.mean(values, axis=-1, keepdims=True)
    centered = values - average
    spread = jnp.mean(centered * centered, axis=-1, keepdims=True)
    return centered * lax.rsqrt(spread + norm_eps) * gain_row


def gather_kernel(routes, index_ref, a_ref, *refs):
    outs, sems = refs[:-1], refs[-1]
    copies = []
    for n, (out, spot) in enumerate(routes):
        copies.append(pltpu.make_async_copy(a_ref.at[index_ref[n]], outs[out].at[spot], sems.at[n]))
    for copy in copies:
        copy.start()
    for copy in copies:
        copy.wait()


def gather_pieces(arrivals, owner_map, rings, together, dates):
    slots, strip, width = arrivals.shape
    tiles = slots // dates
    date, tile = lax.axis_index("date"), lax.axis_index("tile")
    routes, order = [], []
    for s in rings + together:
        for m in range(dates):
            order.append((s, m))
            routes.append((rings.index(s), m) if s in rings else (len(rings) + m, together.index(s)))
    s_of = jnp.array([s for s, _ in order], jnp.int32)
    m_of = jnp.array([m for _, m in order], jnp.int32)
    wanted = (date ^ m_of) * tiles + (tile ^ s_of)
    spots = jnp.arange(slots, dtype=jnp.int32)[None, :]
    index = jnp.sum(jnp.where(owner_map[None, :] == wanted[:, None], spots, 0), axis=1)
    shapes = [jax.ShapeDtypeStruct((dates, strip, width), bf16)] * len(rings)
    shapes += [jax.ShapeDtypeStruct((len(together), strip, width), bf16)] * dates
    anywhere = pl.BlockSpec(memory_space=pl.ANY)
    outs = pl.pallas_call(
        functools.partial(gather_kernel, routes),
        in_specs=[pl.BlockSpec(memory_space=pltpu.SMEM), pl.BlockSpec(memory_space=pltpu.VMEM)],
        out_specs=[anywhere] * len(shapes),
        out_shape=shapes,
        scratch_shapes=[pltpu.SemaphoreType.DMA((len(routes),))],
        compiler_params=pltpu.CompilerParams(vmem_limit_bytes=4 * 2**20),
        cost_estimate=pl.CostEstimate(flops=0, bytes_accessed=0, transcendentals=0),
        name="gather_pieces",
    )(index, arrivals)
    return outs[: len(rings)], outs[len(rings) :]


def swap(value, axis, mask):
    return lax.ppermute(value, axis, [(i, i ^ mask) for i in range(lax.axis_size(axis))])


def exchange(arrivals, owner_map, prepare, use):
    dates, tiles = lax.axis_size("date"), lax.axis_size("tile")
    half, late = tiles // 2, tiles - max(1, tiles // 4)
    rings, mixed = gather_pieces(arrivals, owner_map, list(range(1, late)), list(range(late, tiles)), dates)
    rings = [swap(ring, "tile", s) for s, ring in enumerate(rings, 1)]
    mixed = [value if m == 0 else swap(value, "date", m) for m, value in enumerate(mixed)]
    stacked = [jnp.stack([value[i] for value in mixed]) for i in range(tiles - late)]
    arrivals, stacked = lax.optimization_barrier((arrivals, stacked))
    last = [(swap(pieces, "tile", late + i), None) for i, pieces in enumerate(stacked)]
    _, own = gather_pieces(arrivals, owner_map, [], [0], dates)
    own = [value if m == 0 else swap(value, "date", m) for m, value in enumerate(own)]
    prepared = prepare(stacked)
    close, far = rings[: half - 1], rings[half - 1 :]
    close, prepared = lax.optimization_barrier((close, prepared))

    def cross_dates(ring):
        return [(ring if m == 0 else swap(ring[m : m + 1], "date", m), 0) for m in range(dates)]

    near = [(value, 0) for value in own]
    for ring in close:
        near += cross_dates(ring)
    arrays, far = lax.optimization_barrier(([array for array, _ in near], far))
    near = [(array, n) for array, (_, n) in zip(arrays, near)]
    for ring in far:
        last += cross_dates(ring)
    return use(near, prepared), last, prepared


def with_ones(values):
    return jnp.concatenate([values, jnp.ones((SUM_ROWS, values.shape[1]), bf16)], axis=0)


def normalize(x, loc_ref, gain_ref):
    return layer_norm(x.astype(f32) + loc_ref[...], gain_ref[...].astype(f32)).astype(bf16)


def project_block(weight_ref, normed, packed_ref, norm_ref):
    width = weight_ref.shape[0]
    block = width // 2
    heads = HEADS // 2
    for first in range(0, weight_ref.shape[1], block):
        packed = mm(weight_ref[:, first : first + block], normed, (((0,), (1,)), ((), ()))).astype(bf16)
        packed_ref[first : first + block, :] = packed
        if first < 2 * width:
            packed = packed.astype(f32)
            squares = jnp.sum((packed * packed).reshape(heads, block // heads, packed.shape[1]), axis=1)
            largest = jnp.max(squares, axis=1, keepdims=True)
            row = first // block * heads
            norm_ref[row : row + heads, :] = jnp.broadcast_to(largest, (heads, norm_ref.shape[1]))


def project_kernel(places, *refs):
    count = len(places)
    piece_refs, (loc_ref, gain_ref, weight_ref, packed_ref, norm_ref, x_ref, normed_ref) = refs[:count], refs[count:]
    first = 0
    for piece_ref, place in zip(piece_refs, places):
        x = piece_ref[place]
        x_ref[first : first + x.shape[0], :] = x
        normed_ref[first : first + x.shape[0], :] = normalize(x, loc_ref, gain_ref)
        first += x.shape[0]
    project_block(weight_ref, normed_ref[...], packed_ref, norm_ref)


def project(pieces, location, gain, weight):
    width = weight.shape[0]
    tokens = sum(piece.shape[1] for piece, _ in pieces)
    whole = pl.BlockSpec(memory_space=pltpu.VMEM)
    specs = [pl.BlockSpec((1,) + piece.shape[1:], lambda i: (0, 0, 0)) for piece, _ in pieces]
    return pl.pallas_call(
        functools.partial(project_kernel, [n for _, n in pieces]),
        grid=(1,),
        in_specs=specs + [whole] * 3,
        out_specs=[whole] * 3,
        out_shape=[
            jax.ShapeDtypeStruct((weight.shape[1], tokens), bf16),
            jax.ShapeDtypeStruct((2 * HEADS, 128), f32),
            jax.ShapeDtypeStruct((tokens, width), bf16),
        ],
        scratch_shapes=[pltpu.VMEM((tokens, width), bf16)],
        compiler_params=pltpu.CompilerParams(vmem_limit_bytes=16 * 2**20),
        cost_estimate=pl.CostEstimate(flops=0, bytes_accessed=0, transcendentals=0),
        name="project",
    )(*[piece for piece, _ in pieces], location, gain, weight)


def encode_kernel(places, order, place_ref, packed_ref, norm_ref, x_ref, *refs):
    count = len(places)
    piece_refs, refs = refs[:count], refs[count:]
    (
        loc_ref, gain_ref, weight_ref, out_ref, final_ref, wr_ref, bias_ref, profile_ref,
        o_ref, last_ref, first_ref, tail_ref, normed_ref, rest_ref, rest_norm_ref, mixed_ref, encoded_ref, reduced_ref
    ) = refs
    first = 0
    for piece_ref, n in zip(piece_refs, places):
        x = piece_ref[...].reshape(-1, piece_ref.shape[-1]) if n is None else piece_ref[0]
        tail_ref[first : first + x.shape[0], :] = x
        normed_ref[first : first + x.shape[0], :] = normalize(x, loc_ref, gain_ref)
        first += x.shape[0]
    width = weight_ref.shape[0]
    head = width // HEADS
    scale = math.log2(math.e) / math.sqrt(head)
    project_block(weight_ref, normed_ref[...], rest_ref, rest_norm_ref)
    packed_refs = (packed_ref, rest_ref)
    norms = jnp.maximum(norm_ref[...], rest_norm_ref[...])
    small = jnp.max(norms[:HEADS] * norms[HEADS:]) <= (EXPONENT_BOUND / scale) ** 2

    def side_by_side(which, n):
        rows = pl.ds(pl.multiple_of(which * width + n * head, 16), head)
        return jnp.concatenate([ref[rows, :] for ref in packed_refs], axis=1)

    def scores(n):
        return mm(side_by_side(1, n), side_by_side(0, n), TN)

    def finish(n, lifted):
        sums = mm(with_ones(side_by_side(2, n)), lifted.astype(bf16))
        rows = pl.ds(pl.multiple_of(n * head, 16), head)
        mixed_ref[rows, :] = (sums[:head] * (1.0 / sums[head : head + 1])).astype(bf16)

    @pl.when(small)
    def _():
        def heads(pair, carry):
            for n in range(PAIR):
                finish(pair * PAIR + n, jnp.exp2(scores(pair * PAIR + n) * scale))
            return carry

        lax.fori_loop(0, HEADS // PAIR, heads, 0)

    @pl.when(jnp.logical_not(small))
    def _():
        def heads(n, carry):
            held = scores(n)
            finish(n, jnp.exp2((held - jnp.max(held, axis=0, keepdims=True)) * scale))
            return carry

        lax.fori_loop(0, HEADS, heads, 0)

    tiles, dates, strip, _ = encoded_ref.shape
    first = 0
    step = tiles * dates * strip // 4
    for held_ref in (x_ref, tail_ref):
        for row in range(0, held_ref.shape[0], step):
            held = held_ref[row : row + step, :].astype(f32) + loc_ref[...]
            updated = held + mm(mixed_ref[:, first : first + step], out_ref[...], TN)
            encoded = layer_norm(updated, final_ref[...].astype(f32)).astype(bf16)
            part = step // (dates * strip)
            group = first // (dates * strip)
            encoded_ref[group : group + part] = encoded.reshape(part, dates, strip, width)
            first += step
    total = bias_ref[...].astype(f32)
    for m in range(dates):
        total = total + mm(encoded_ref[:, m].reshape(tiles * strip, width), wr_ref[place_ref[0] ^ m])
    total = 0.5 * total * (1.0 + lax.erf(total * math.sqrt(0.5)))
    halves = range(reduced_ref.shape[0])
    for n, s in enumerate(order):
        spot = pl.multiple_of((place_ref[1] ^ s) * strip, strip)
        for half in halves:
            lanes = slice(128 * half, 128 * (half + 1))
            reduced_ref[half, pl.ds(spot, strip), :] = total[n * strip : (n + 1) * strip, lanes]
    for half in halves:
        o_ref[:, 128 * half : 128 * (half + 1)] = reduced_ref[half].astype(bf16)

    def column(b):
        return jnp.concatenate([reduced_ref[half, pl.ds(b, PATCHES, stride=PATCHES), :] for half in halves], axis=1)

    tail = jnp.zeros((PATCHES - 2, o_ref.shape[1]), f32)
    tail = jnp.concatenate([profile_ref[...].astype(f32), tail], axis=0)
    is_last = place_ref[2] == 1
    sent = [jnp.where(is_last, column(PATCHES - 2 + i), column(i)) for i in range(2)]
    last_ref[...] = jnp.concatenate(sent + [tail], axis=0).astype(bf16)
    first_ref[...] = jnp.concatenate([column(0), column(1), tail], axis=0).astype(bf16)


def encode(
    place, packed, norms, x, last, location, gain, weight, out_weight, final_gain, reduce_weight, reduce_bias, profile,
    tiles, dates
):
    width = weight.shape[0]
    tokens = 2 * x.shape[0]
    rest = tokens - x.shape[0]
    strip = tokens // (tiles * dates)
    dec = reduce_weight.shape[1]
    patches = tiles * strip
    quarter = tiles // 4
    order = list(range(2 * quarter)) + list(range(3 * quarter, tiles)) + list(range(2 * quarter, 3 * quarter))
    sent = jax.ShapeDtypeStruct((3 * PATCHES, dec), bf16)
    whole = pl.BlockSpec(memory_space=pltpu.VMEM)
    pieces = [
        pl.BlockSpec(piece.shape if n is None else (1,) + piece.shape[1:], lambda i: (0, 0, 0)) for piece, n in last
    ]
    return pl.pallas_call(
        functools.partial(encode_kernel, [n for _, n in last], order),
        grid=(1,),
        in_specs=[pl.BlockSpec(memory_space=pltpu.SMEM)] + [whole] * 3 + pieces + [whole] * 8,
        out_specs=[whole] * 3,
        out_shape=[jax.ShapeDtypeStruct((patches, dec), bf16), sent, sent],
        scratch_shapes=[
            pltpu.VMEM((rest, width), bf16),
            pltpu.VMEM((rest, width), bf16),
            pltpu.VMEM((3 * width, rest), bf16),
            pltpu.VMEM((2 * HEADS, 128), f32),
            pltpu.VMEM((width, tokens), bf16),
            pltpu.VMEM((tiles, dates, strip, width), bf16),
            pltpu.VMEM((dec // 128, patches, 128), f32),
        ],
        compiler_params=pltpu.CompilerParams(vmem_limit_bytes=36 * 2**20),
        name="encode",
    )(
        place, packed, norms, x, *[piece for piece, _ in last], location, gain, weight, out_weight, final_gain,
        reduce_weight.reshape(dates, width, dec), reduce_bias, profile,
    )


FIRST_OWN = RIM // PATCH
LAST_OWN = PATCHES - 1 - FIRST_OWN
UPPER = [a for a in range(PATCHES) if PATCH * a + PATCH >= TILE_PX - RIM]
LOWER = [a for a in range(PATCHES) if PATCH * a - 1 < RIM]
ENTRIES = (
    [(0, a) for a in UPPER]
    + [(0, None)]
    + [(1, a) for a in range(FIRST_OWN, LAST_OWN + 1)]
    + [(2, a) for a in LOWER]
    + [(2, None)]
)
SIDE = 16


def placement():
    main = np.zeros((3, SPAN, PATCHES, STRIDE), np.float32)
    side = np.zeros((3, SIDE, STRIDE), np.float32)
    for j in range(SPAN):
        for slot in range(PATCHES):
            if slot == 0:
                which, x = 0, PATCH * (PATCHES - 1) + j - 1
            elif slot == PATCHES - 1:
                which, x = 2, j - 1
            else:
                which, x = 1, PATCH * slot + j - 1
            column = x + (which - 1) * STRIDE - RIM
            if 0 <= x < TILE_PX and 0 <= column < STRIDE:
                main[which, j, slot, column] = 1.0
    rows = []
    for j in range(SPAN):
        x = PATCH * (PATCHES - 2) + j - 1
        if TILE_PX - RIM <= x < TILE_PX:
            side[0, len(rows), x - (TILE_PX - RIM)] = 1.0
            rows.append((0, j))
    for j in range(SPAN):
        x = PATCH + j - 1
        if 0 <= x < RIM:
            side[2, len(rows), STRIDE - RIM + x] = 1.0
            rows.append((2, j))
    side[0, len(rows), RIM - 1] = 1.0
    side[2, len(rows) + 1, STRIDE - RIM] = 1.0
    return main.reshape(3, SPAN * PATCHES, STRIDE), side, rows


PLACE_MAIN, PLACE_SIDE, SIDE_ROWS = placement()


def windows():
    table = np.zeros((3, LANES, STRIDE), np.float32)
    for x in range(STRIDE):
        table[1, x + RIM, x] = 1.0
    for x in range(RIM):
        table[0, TILE_PX - RIM + x, x] = 1.0
        table[2, x, STRIDE - RIM + x] = 1.0
    return table


def row_lanes(classes):
    table = np.zeros((LANES, len(ENTRIES), LANES), np.float32)
    for n, (tile_row, a) in enumerate(ENTRIES):
        for k in range(classes):
            if a is None:
                halo = classes * SPAN + k + (classes if tile_row == 0 else 0)
                table[TILE_PX - 1 if tile_row == 0 else 0, n, halo] = 1.0
                continue
            for i in range(SPAN):
                y = PATCH * a - 1 + i
                if 0 <= y < TILE_PX:
                    table[y, n, k * SPAN + i] = 1.0
    return table.reshape(LANES, -1)


def tap_tables(classes):
    rows = np.zeros((LANES, classes), np.float32)
    columns = np.zeros((FEAT, FEAT * PATCH), np.float32)
    meet = np.zeros((3, LANES, FEAT, PATCH), np.float32)
    for f in range(FEAT):
        columns[f, f * PATCH : (f + 1) * PATCH] = 1.0
    for k in range(classes):
        rows[k * SPAN : (k + 1) * SPAN, k] = 1.0
        rows[classes * SPAN + k, k] = 1.0
        rows[classes * (SPAN + 1) + k, k] = 1.0
        for dy in range(3):
            for i in range(PATCH):
                meet[dy, k * SPAN + i + 2 - dy, :, i] = 1.0
        meet[0, classes * SPAN + k, :, FAR_PIXEL] = 1.0
        meet[2, classes * (SPAN + 1) + k, :, NEAR_PIXEL] = 1.0
    return rows, columns, meet.reshape(3, LANES, FEAT * PATCH)


def kernels_kernel(up_ref, taps_ref, rows_ref, columns_ref, meet_ref, o_ref, edge_ref, turned_ref, column_ref):
    for half in range(turned_ref.shape[0]):
        lanes = slice(128 * half, 128 * (half + 1))
        turned_ref[half] = up_ref[lanes, :].astype(f32).T
        for j in range(PATCH):
            column_ref[j, :, lanes] = turned_ref[half, pl.ds(j, FEAT * PATCH, stride=PATCH), :].astype(bf16)
    spread = []
    for dx in range(3):
        total = None
        for dy in range(3):
            taps = mm(mm(rows_ref[...], taps_ref[3 * dy + dx]).astype(bf16), columns_ref[...])
            part = taps * meet_ref[dy].astype(f32)
            total = part if total is None else total + part
        spread.append(total.astype(bf16))
    for big in range(SPAN):
        total = None
        for dx in range(3):
            j = big - 2 + dx
            if 0 <= j < PATCH:
                part = mm(spread[dx], column_ref[j])
                total = part if total is None else total + part
        o_ref[big] = total.astype(bf16)
    edge_ref[0] = mm(spread[2], column_ref[NEAR_PIXEL]).astype(bf16)
    edge_ref[1] = mm(spread[0], column_ref[FAR_PIXEL]).astype(bf16)


def decoder_kernels(upsample_weight, class_weight):
    channels = upsample_weight.shape[0]
    tables = [jnp.asarray(table, bf16) for table in tap_tables(class_weight.shape[1])]
    return pl.pallas_call(
        kernels_kernel,
        out_shape=[
            jax.ShapeDtypeStruct((SPAN, LANES, channels), bf16),
            jax.ShapeDtypeStruct((2, LANES, channels), bf16),
        ],
        scratch_shapes=[
            pltpu.VMEM((channels // 128, upsample_weight.shape[1], 128), f32),
            pltpu.VMEM((PATCH, FEAT * PATCH, channels), bf16),
        ],
        compiler_params=pltpu.CompilerParams(vmem_limit_bytes=VMEM),
        cost_estimate=pl.CostEstimate(flops=0, bytes_accessed=0, transcendentals=0),
        name="decoder_kernels",
    )(upsample_weight, class_weight, *tables)


def compose_kernel(
    classes, own_ref, before_ref, after_ref, above_ref, below_ref, profile_ref, m_ref, edge_ref,
    lanes_ref, window_ref, place_ref, side_ref, bias_ref,
    o_ref, a_ref, b_ref, z_ref, z2_ref, acc_ref
):
    count = len(ENTRIES)
    edge = len(UPPER)
    own, before, after, above, below = (
        ref[...].astype(f32) for ref in (own_ref, before_ref, after_ref, above_ref, below_ref)
    )
    slot = lax.broadcasted_iota(jnp.int32, (PATCHES, LANES), 0)

    def line(tile_row, a):
        if tile_row == 1 or a is None:
            a = a if a is not None else (NEAR_PATCH if tile_row == 0 else FAR_PATCH)
            sides = [before[a : a + 1], before[PATCHES + a : PATCHES + a + 1]]
            sides += [after[a : a + 1], after[PATCHES + a : PATCHES + a + 1]]
            return own[PATCHES * a : PATCHES * (a + 1)], sides
        source = above if tile_row == 0 else below
        n = (UPPER if tile_row == 0 else LOWER).index(a)
        first = PATCHES * edge + 4 * n
        return source[PATCHES * n : PATCHES * (n + 1)], [source[first + i : first + i + 1] for i in range(4)]

    def slots(rows, base):
        for i, row in rows.items():
            base = jnp.where(slot == i, row, base)
        return base

    def second(before_row, after_row, near, far):
        rows = {i: before_row if which == 0 else after_row for i, (which, _) in enumerate(SIDE_ROWS)}
        rows[len(SIDE_ROWS)] = near
        rows[len(SIDE_ROWS) + 1] = far
        return slots(rows, jnp.zeros((SIDE, LANES), f32))

    profile = profile_ref[...].astype(f32)
    tail = slice(2 * PATCHES, 2 * PATCHES + 2)
    ends = slice((PATCHES + 4) * edge, (PATCHES + 4) * edge + 6)
    profiles = jnp.concatenate([above[ends], before[tail], profile, after[tail], below[ends]], axis=0)
    row_profiles = [profiles[2 * i : 2 * i + 1] for i in range(9)]
    col_profiles = [profiles[2 * i + 1 : 2 * i + 2] for i in range(9)]
    blank = jnp.zeros((PATCHES - 9, LANES), f32)
    row_table = jnp.concatenate(row_profiles + [blank], axis=0).astype(bf16)
    col_table = jnp.concatenate(col_profiles + [blank], axis=0).astype(bf16)
    weights = mm(row_table, lanes_ref[...])
    rows = [mm(row_table, window_ref[i]) for i in range(3)]
    cols = [mm(col_table, window_ref[i]) for i in range(3)]
    block_rows = jnp.concatenate([rows[i // 3][i : i + 1] for i in range(9)] + [blank[:, :STRIDE]], axis=0)
    block_cols = jnp.concatenate([cols[i % 3][i : i + 1] for i in range(9)] + [blank[:, :STRIDE]], axis=0)
    den = mm(block_rows.astype(bf16), block_cols.astype(bf16), TN)
    spots, side_spots = [], []
    for tile_row in range(3):
        spots.append(sum(place_ref[i].astype(f32) * block_cols[3 * tile_row + i][None] for i in range(3)).astype(bf16))
        side_spots.append(
            sum(side_ref[i].astype(f32) * block_cols[3 * tile_row + i][None] for i in range(3)).astype(bf16)
        )

    def entry_weights(n, tile_row):
        return [weights[3 * tile_row + i : 3 * tile_row + i + 1, LANES * n : LANES * (n + 1)] for i in range(3)]

    main_weights, side_weights = [], []
    for n, (tile_row, a) in enumerate(ENTRIES):
        patches, (l_far, l_near, r_near, r_far) = line(tile_row, a)
        a_ref[n] = slots({0: l_near, PATCHES - 1: r_near}, patches).astype(bf16)
        b_ref[n] = second(
            l_far, r_far, patches[NEAR_PATCH : NEAR_PATCH + 1], patches[FAR_PATCH : FAR_PATCH + 1]
        ).astype(bf16)
        left, middle, right = entry_weights(n, tile_row)
        main_weights.append(slots({0: left, PATCHES - 1: right}, jnp.broadcast_to(middle, (PATCHES, LANES))))
        side_weights.append(second(left, right, left, right))
    main_weights = jnp.stack(main_weights)
    for j in range(SPAN):
        z = mm(a_ref[...].reshape(count * PATCHES, LANES), m_ref[j], NT).reshape(count, PATCHES, LANES)
        z_ref[:, j] = (z * main_weights).astype(bf16)
    side_slot = lax.broadcasted_iota(jnp.int32, (count, SIDE, LANES), 1)
    patches = b_ref[...].astype(f32)
    total = None
    for i in range(len(SIDE_ROWS) + 2):
        kernel = m_ref[SIDE_ROWS[i][1]] if i < len(SIDE_ROWS) else edge_ref[i - len(SIDE_ROWS)]
        part = jnp.where(side_slot == i, patches, 0.0).astype(bf16).reshape(count * SIDE, LANES)
        part = mm(part, kernel, NT)
        total = part if total is None else total + part
    z2_ref[...] = (total.reshape(count, SIDE, LANES) * jnp.stack(side_weights)).astype(bf16)

    acc_ref[...] = jnp.zeros_like(acc_ref)
    for n, (tile_row, a) in enumerate(ENTRIES):
        part = mm(z_ref[n].reshape(SPAN * PATCHES, LANES), spots[tile_row], TN)
        part += mm(z2_ref[n], side_spots[tile_row], TN)
        if a is None:
            first = classes * SPAN + (classes if tile_row == 0 else 0)
            y = 2 * RIM - 1 if tile_row == 0 else STRIDE
            for k in range(classes):
                acc_ref[k, y : y + 1, :] += part[first + k : first + k + 1]
            continue
        y = PATCH * a - 1 + (tile_row - 1) * STRIDE
        low, high = 0, SPAN
        if tile_row == 0:
            high = min(SPAN, TILE_PX - (PATCH * a - 1))
        if tile_row == 2:
            low = max(0, 1 - PATCH * a)
        for k in range(classes):
            acc_ref[k, y + low : y + high, :] += part[k * SPAN + low : k * SPAN + high]
    inverse = 1.0 / jnp.maximum(den, 1.0)
    for k in range(classes):
        o_ref[k] = (acc_ref[k, RIM : RIM + STRIDE, :] + bias_ref[k] * den) * inverse


def forward(size):
    return [(i, i + 1) for i in range(size - 1)]


def backward(size):
    return [(i + 1, i) for i in range(size - 1)]


def exchange_rims(reduced, last, first, profile):
    cols = lax.axis_size("col")
    if cols == 2:
        other = swap(last, "col", 1)
        at_end = lax.axis_index("col") == 1
        before, after = jnp.where(at_end, other, 0), jnp.where(at_end, 0, other)
    else:
        before = lax.ppermute(last, "col", forward(cols))
        after = lax.ppermute(first, "col", backward(cols))

    def lines(rows):
        parts = [reduced[PATCHES * a : PATCHES * (a + 1)] for a in rows]
        for a in rows:
            for side in (before, after):
                parts += [side[a : a + 1], side[PATCHES + a : PATCHES + a + 1]]
        parts += [before[2 * PATCHES : 2 * PATCHES + 2], profile, after[2 * PATCHES : 2 * PATCHES + 2]]
        used = (PATCHES + 4) * len(rows) + 6
        parts.append(jnp.zeros((-used % 16, reduced.shape[1]), bf16))
        return jnp.concatenate(parts, axis=0)

    rows = lax.axis_size("date") * lax.axis_size("tile")
    above = lax.ppermute(lines(UPPER), ("date", "tile"), forward(rows))
    below = lax.ppermute(lines(LOWER), ("date", "tile"), backward(rows))
    return before, after, above, below


def compose(reduced, rims, profile, kernels, edges, class_bias, classes):
    channels = reduced.shape[1]
    count = len(ENTRIES)
    whole = pl.BlockSpec(memory_space=pltpu.VMEM)
    tables = [jnp.asarray(t, bf16) for t in (row_lanes(classes), windows(), PLACE_MAIN, PLACE_SIDE)]
    return pl.pallas_call(
        functools.partial(compose_kernel, classes),
        in_specs=[whole] * 12 + [pl.BlockSpec(memory_space=pltpu.SMEM)],
        out_specs=whole,
        out_shape=jax.ShapeDtypeStruct((classes, STRIDE, STRIDE), f32),
        scratch_shapes=[
            pltpu.VMEM((count, PATCHES, channels), bf16),
            pltpu.VMEM((count, SIDE, channels), bf16),
            pltpu.VMEM((count, SPAN, PATCHES, LANES), bf16),
            pltpu.VMEM((count, SIDE, LANES), bf16),
            pltpu.VMEM((classes, TILE_PX, STRIDE), f32),
        ],
        compiler_params=pltpu.CompilerParams(vmem_limit_bytes=VMEM),
        name="compose",
    )(reduced, *rims, profile, kernels, edges, *tables, class_bias.astype(f32))


def local(
    arrivals,
    owner_map,
    block_ids,
    tile_valid,
    blend_weights,
    location_table,
    norm_gain,
    qkv_weight,
    out_weight,
    final_gain,
    reduce_weight,
    reduce_bias,
    upsample_weight,
    class_weight,
    class_bias,
):
    width = arrivals.shape[-1]
    slots = arrivals.shape[1]
    classes = class_weight.shape[1]
    dates, tiles = lax.axis_size("date"), lax.axis_size("tile")
    codes = block_ids.reshape(1, 1)
    one_hot = (codes == jnp.arange(location_table.shape[0], dtype=jnp.int32)[None, :]).astype(bf16)

    def prepare(stacked):
        table, blend, up, _ = lax.optimization_barrier((location_table, blend_weights, upsample_weight, stacked))
        location = jnp.dot(one_hot, table, preferred_element_type=f32)
        profile = blend.reshape(2, TILE_PX).astype(bf16)
        profile = jnp.concatenate([profile[:1] * tile_valid.reshape(1).astype(bf16), profile[1:]], axis=0)
        profile = jnp.pad(profile, ((0, 0), (0, LANES - TILE_PX)))
        return (location, profile) + tuple(decoder_kernels(up, class_weight))

    def use(pieces, prepared):
        return project(pieces, prepared[0], norm_gain[None], qkv_weight)

    (packed, norms, x), last, prepared = exchange(arrivals.reshape(slots, -1, width), owner_map[0], prepare, use)
    location, profile, kernels, edges = prepared
    go_last = jnp.where((lax.axis_index("col") == 0) | (lax.axis_size("col") != 2), 1, 0)
    place = jnp.stack([lax.axis_index("date"), lax.axis_index("tile"), go_last]).astype(jnp.int32)
    reduced, to_after, to_before = encode(
        place, packed, norms, x, last, location, norm_gain[None], qkv_weight, out_weight, final_gain[None],
        reduce_weight, reduce_bias[None], profile, tiles, dates
    )
    rims = exchange_rims(reduced, to_after, to_before, profile)
    return compose(reduced, rims, profile, kernels, edges, class_bias, classes)[None]


def solution(mesh):
    placed = (
        P(None, None, "col", "date", "tile", None, None),
        P(),
        P(None, ("date", "tile"), "col"),
        P(None, ("date", "tile"), "col"),
        P(None, ("date", "tile"), "col", None, None),
    ) + (P(),) * 10
    return jax.shard_map(
        local,
        mesh=mesh,
        in_specs=placed,
        out_specs=P(None, None, ("date", "tile"), "col"),
        check_vma=False,
    )
```

```python
import functools
import math

import jax
import jax.numpy as jnp
import numpy as np
from jax import lax
from jax.experimental import pallas as pl
from jax.experimental.pallas import tpu as pltpu
from jax.sharding import PartitionSpec as P

HEADS = 16
DATES = 4
PATCH = 14
INTERSECTION = 32
FEAT = 16
PATCHES = 16
RIM = 16
TILE_PX = PATCH * PATCHES
STRIDE = TILE_PX - INTERSECTION
SPAN = PATCH + 2
FAR_PATCH, FAR_PIXEL = divmod(STRIDE - 1, PATCH)
NEAR_PATCH, NEAR_PIXEL = divmod(INTERSECTION, PATCH)
LANES = 256
VMEM = 56 * 2**20

EXPONENT_BOUND = 100.0
SUM_ROWS = 16
PAIR = 2
GROUP = 256

norm_eps = 1e-06
bf16 = jnp.bfloat16
f32 = jnp.float32

NN = (((1,), (0,)), ((), ()))
NT = (((1,), (1,)), ((), ()))
TN = (((0,), (0,)), ((), ()))


def mm(left, right, dims=NN):
    return lax.dot_general(left, right, dims, preferred_element_type=f32)


def layer_norm(values, gain_row):
    average = jnp.mean(values, axis=-1, keepdims=True)
    centered = values - average
    spread = jnp.mean(centered * centered, axis=-1, keepdims=True)
    return centered * lax.rsqrt(spread + norm_eps) * gain_row


def gather_kernel(dates, tiles, routes, owner_ref, a_ref, *refs):
    outs, slot_ref = refs[:-1], refs[-1]
    for slot in range(dates * tiles):
        slot_ref[owner_ref[slot]] = slot
    date, tile = lax.axis_index("date"), lax.axis_index("tile")
    for s, m, out, spot in routes:
        outs[out][spot] = a_ref[slot_ref[(date ^ m) * tiles + (tile ^ s)]]


def gather_pieces(arrivals, owner_map, groups, dates):
    slots, strip, width = arrivals.shape
    routes = [(s, m, n, i) for n, group in enumerate(groups) for i, (s, m) in enumerate(group)]
    whole = pl.BlockSpec(memory_space=pltpu.VMEM)
    return pl.pallas_call(
        functools.partial(gather_kernel, dates, slots // dates, routes),
        in_specs=[pl.BlockSpec(memory_space=pltpu.SMEM), whole],
        out_specs=[whole] * len(groups),
        out_shape=[pltpu.VMEM((len(group), strip, width), bf16) for group in groups],
        scratch_shapes=[pltpu.SMEM((slots,), jnp.int32)],
        compiler_params=pltpu.CompilerParams(vmem_limit_bytes=12 * 2**20),
        cost_estimate=pl.CostEstimate(flops=0, bytes_accessed=0, transcendentals=0),
        name="gather_pieces",
    )(owner_map, arrivals)


def swap(value, axis, mask):
    return lax.ppermute(value, axis, [(i, i ^ mask) for i in range(lax.axis_size(axis))])


def exchange(arrivals, owner_map, prepare, use):
    dates, tiles = lax.axis_size("date"), lax.axis_size("tile")
    half, late = tiles // 2, tiles - max(1, tiles // 4)
    groups = [[(s, m) for m in range(dates)] for s in range(1, late)]
    groups += [[(s, m) for s in range(late, tiles)] for m in range(dates)]
    groups += [[(0, m)] for m in range(dates)]
    pieces = gather_pieces(arrivals, owner_map, groups, dates)
    rings, mixed, own = pieces[: late - 1], pieces[late - 1 : -dates], pieces[-dates:]
    far = [swap(ring, "tile", s) for s, ring in enumerate(rings[half - 1 :], half)]
    mixed = [value if m == 0 else swap(value, "date", m) for m, value in enumerate(mixed)]
    last = [jnp.stack([value[i] for value in mixed]) for i in range(tiles - late)]
    own, last = lax.optimization_barrier((own, last))
    close = [swap(ring, "tile", s) for s, ring in enumerate(rings[: half - 1], 1)]
    own = [value if m == 0 else swap(value, "date", m) for m, value in enumerate(own)]
    prepared = prepare(last)
    far, last, first = lax.optimization_barrier((far, last, prepared[0]))
    prepared = (first,) + prepared[1:]
    last = [(swap(pieces, "tile", s), None) for s, pieces in enumerate(last, late)]

    def cross_dates(ring):
        return [(ring if m == 0 else swap(ring[m : m + 1], "date", m), 0) for m in range(dates)]

    near = [(value, 0) for value in own]
    for ring in close:
        near += cross_dates(ring)
    middle = []
    for ring in far:
        middle += cross_dates(ring)
    return zip(*[use(pieces, prepared) for pieces in (near, middle, last)]), prepared


def with_ones(values):
    return jnp.concatenate([values, jnp.ones((SUM_ROWS, values.shape[1]), bf16)], axis=0)


def normalize(x, loc_ref, gain_ref):
    return layer_norm(x.astype(f32) + loc_ref[...], gain_ref[...].astype(f32)).astype(bf16)


def project_block(weight_ref, normed, packed_ref, norm_ref):
    width = weight_ref.shape[0]
    block = width // 2
    heads = HEADS // 2
    for first in range(0, weight_ref.shape[1], block):
        packed = mm(weight_ref[:, first : first + block], normed, (((0,), (1,)), ((), ()))).astype(bf16)
        packed_ref[first : first + block, :] = packed
        if first < 2 * width:
            packed = packed.astype(f32)
            squares = jnp.sum((packed * packed).reshape(heads, block // heads, packed.shape[1]), axis=1)
            largest = jnp.max(squares, axis=1, keepdims=True)
            row = first // block * heads
            norm_ref[row : row + heads, :] = jnp.broadcast_to(largest, (heads, norm_ref.shape[1]))


def project_kernel(places, *refs):
    count = len(places)
    piece_refs, (loc_ref, gain_ref, weight_ref, packed_ref, norm_ref, x_ref, normed_ref) = refs[:count], refs[count:]
    first = 0
    for piece_ref, place in zip(piece_refs, places):
        x = piece_ref[...].reshape(-1, piece_ref.shape[-1]) if place is None else piece_ref[place]
        x_ref[first : first + x.shape[0], :] = x
        normed_ref[first : first + x.shape[0], :] = normalize(x, loc_ref, gain_ref)
        first += x.shape[0]
    project_block(weight_ref, normed_ref[...], packed_ref, norm_ref)


def project(pieces, location, gain, weight):
    width = weight.shape[0]
    tokens = sum(piece.shape[1] * (piece.shape[0] if n is None else 1) for piece, n in pieces)
    whole = pl.BlockSpec(memory_space=pltpu.VMEM)
    specs = [
        pl.BlockSpec(piece.shape if n is None else (1,) + piece.shape[1:], lambda i: (0, 0, 0)) for piece, n in pieces
    ]
    return pl.pallas_call(
        functools.partial(project_kernel, [n for _, n in pieces]),
        grid=(1,),
        in_specs=specs + [whole] * 3,
        out_specs=[whole] * 3,
        out_shape=[
            jax.ShapeDtypeStruct((weight.shape[1], tokens), bf16),
            jax.ShapeDtypeStruct((2 * HEADS, 128), f32),
            jax.ShapeDtypeStruct((tokens, width), bf16),
        ],
        scratch_shapes=[pltpu.VMEM((tokens, width), bf16)],
        compiler_params=pltpu.CompilerParams(vmem_limit_bytes=16 * 2**20),
        cost_estimate=pl.CostEstimate(flops=0, bytes_accessed=0, transcendentals=0),
        name="project",
    )(*[piece for piece, _ in pieces], location, gain, weight)


def encode_kernel(parts, place_ref, *refs):
    packed_refs, norm_refs, x_refs = (refs[i * parts : (i + 1) * parts] for i in range(3))
    (
        loc_ref, out_ref, final_ref, wr_ref, bias_ref, profile_ref,
        o_ref, last_ref, first_ref, mixed_ref, encoded_ref, reduced_ref
    ) = refs[3 * parts :]
    width = out_ref.shape[0]
    head = width // HEADS
    scale = math.log2(math.e) / math.sqrt(head)
    norms = norm_refs[0][...]
    for norm_ref in norm_refs[1:]:
        norms = jnp.maximum(norms, norm_ref[...])
    small = jnp.max(norms[:HEADS] * norms[HEADS:]) <= (EXPONENT_BOUND / scale) ** 2

    def side_by_side(which, n):
        rows = pl.ds(pl.multiple_of(which * width + n * head, 16), head)
        return jnp.concatenate([ref[rows, :] for ref in packed_refs], axis=1)

    def scores(n):
        return mm(side_by_side(1, n), side_by_side(0, n), TN)

    def finish(n, lifted):
        sums = mm(with_ones(side_by_side(2, n)), lifted.astype(bf16))
        rows = pl.ds(pl.multiple_of(n * head, 16), head)
        mixed_ref[rows, :] = (sums[:head] * (1.0 / sums[head : head + 1])).astype(bf16)

    @pl.when(small)
    def _():
        def heads(pair, carry):
            for n in range(PAIR):
                finish(pair * PAIR + n, jnp.exp2(scores(pair * PAIR + n) * scale))
            return carry

        lax.fori_loop(0, HEADS // PAIR, heads, 0)

    @pl.when(jnp.logical_not(small))
    def _():
        def heads(n, carry):
            held = scores(n)
            finish(n, jnp.exp2((held - jnp.max(held, axis=0, keepdims=True)) * scale))
            return carry

        lax.fori_loop(0, HEADS, heads, 0)

    tiles, dates, strip, _ = encoded_ref.shape
    first = 0
    step = tiles * dates * strip // 4
    for held_ref in x_refs:
        for row in range(0, held_ref.shape[0], step):
            held = held_ref[row : row + step, :].astype(f32) + loc_ref[...]
            updated = held + mm(mixed_ref[:, first : first + step], out_ref[...], TN)
            encoded = layer_norm(updated, final_ref[...].astype(f32)).astype(bf16)
            part = step // (dates * strip)
            group = first // (dates * strip)
            encoded_ref[group : group + part] = encoded.reshape(part, dates, strip, width)
            first += step
    total = bias_ref[...].astype(f32)
    for m in range(dates):
        total = total + mm(encoded_ref[:, m].reshape(tiles * strip, width), wr_ref[place_ref[0] ^ m])
    total = 0.5 * total * (1.0 + lax.erf(total * math.sqrt(0.5)))
    halves = range(reduced_ref.shape[0])
    for s in range(tiles):
        spot = pl.multiple_of((place_ref[1] ^ s) * strip, strip)
        for half in halves:
            lanes = slice(128 * half, 128 * (half + 1))
            reduced_ref[half, pl.ds(spot, strip), :] = total[s * strip : (s + 1) * strip, lanes]
    for half in halves:
        o_ref[:, 128 * half : 128 * (half + 1)] = reduced_ref[half].astype(bf16)

    def column(b):
        return jnp.concatenate([reduced_ref[half, pl.ds(b, PATCHES, stride=PATCHES), :] for half in halves], axis=1)

    tail = jnp.zeros((PATCHES - 2, o_ref.shape[1]), f32)
    tail = jnp.concatenate([profile_ref[...].astype(f32), tail], axis=0)
    is_last = place_ref[2] == 1
    sent = [jnp.where(is_last, column(PATCHES - 2 + i), column(i)) for i in range(2)]
    last_ref[...] = jnp.concatenate(sent + [tail], axis=0).astype(bf16)
    first_ref[...] = jnp.concatenate([column(0), column(1), tail], axis=0).astype(bf16)


def encode(
    place, packed, norms, x, location, out_weight, final_gain, reduce_weight, reduce_bias, profile, tiles, dates
):
    width = out_weight.shape[0]
    tokens = sum(part.shape[0] for part in x)
    strip = tokens // (tiles * dates)
    dec = reduce_weight.shape[1]
    patches = tiles * strip
    sent = jax.ShapeDtypeStruct((3 * PATCHES, dec), bf16)
    whole = pl.BlockSpec(memory_space=pltpu.VMEM)
    return pl.pallas_call(
        functools.partial(encode_kernel, len(packed)),
        in_specs=[pl.BlockSpec(memory_space=pltpu.SMEM)] + [whole] * (3 * len(packed) + 6),
        out_specs=[whole] * 3,
        out_shape=[jax.ShapeDtypeStruct((patches, dec), bf16), sent, sent],
        scratch_shapes=[
            pltpu.VMEM((width, tokens), bf16),
            pltpu.VMEM((tiles, dates, strip, width), bf16),
            pltpu.VMEM((dec // 128, patches, 128), f32),
        ],
        compiler_params=pltpu.CompilerParams(vmem_limit_bytes=28 * 2**20),
        name="encode",
    )(
        place, *packed, *norms, *x, location, out_weight, final_gain,
        reduce_weight.reshape(dates, width, dec), reduce_bias, profile,
    )


FIRST_OWN = RIM // PATCH
LAST_OWN = PATCHES - 1 - FIRST_OWN
UPPER = [a for a in range(PATCHES) if PATCH * a + PATCH >= TILE_PX - RIM]
LOWER = [a for a in range(PATCHES) if PATCH * a - 1 < RIM]
ENTRIES = (
    [(0, a) for a in UPPER]
    + [(0, None)]
    + [(1, a) for a in range(FIRST_OWN, LAST_OWN + 1)]
    + [(2, a) for a in LOWER]
    + [(2, None)]
)
SIDE = 16


def placement():
    main = np.zeros((3, SPAN, PATCHES, STRIDE), np.float32)
    side = np.zeros((3, SIDE, STRIDE), np.float32)
    for j in range(SPAN):
        for slot in range(PATCHES):
            if slot == 0:
                which, x = 0, PATCH * (PATCHES - 1) + j - 1
            elif slot == PATCHES - 1:
                which, x = 2, j - 1
            else:
                which, x = 1, PATCH * slot + j - 1
            column = x + (which - 1) * STRIDE - RIM
            if 0 <= x < TILE_PX and 0 <= column < STRIDE:
                main[which, j, slot, column] = 1.0
    rows = []
    for j in range(SPAN):
        x = PATCH * (PATCHES - 2) + j - 1
        if TILE_PX - RIM <= x < TILE_PX:
            side[0, len(rows), x - (TILE_PX - RIM)] = 1.0
            rows.append((0, j))
    for j in range(SPAN):
        x = PATCH + j - 1
        if 0 <= x < RIM:
            side[2, len(rows), STRIDE - RIM + x] = 1.0
            rows.append((2, j))
    side[0, len(rows), RIM - 1] = 1.0
    side[2, len(rows) + 1, STRIDE - RIM] = 1.0
    return main.reshape(3, SPAN * PATCHES, STRIDE), side, rows


PLACE_MAIN, PLACE_SIDE, SIDE_ROWS = placement()


def windows():
    table = np.zeros((3, LANES, STRIDE), np.float32)
    for x in range(STRIDE):
        table[1, x + RIM, x] = 1.0
    for x in range(RIM):
        table[0, TILE_PX - RIM + x, x] = 1.0
        table[2, x, STRIDE - RIM + x] = 1.0
    return table


def row_lanes(classes):
    table = np.zeros((LANES, len(ENTRIES), LANES), np.float32)
    for n, (tile_row, a) in enumerate(ENTRIES):
        for k in range(classes):
            if a is None:
                halo = classes * SPAN + k + (classes if tile_row == 0 else 0)
                table[TILE_PX - 1 if tile_row == 0 else 0, n, halo] = 1.0
                continue
            for i in range(SPAN):
                y = PATCH * a - 1 + i
                if 0 <= y < TILE_PX:
                    table[y, n, k * SPAN + i] = 1.0
    return table.reshape(LANES, -1)


def tap_tables(classes):
    rows = np.zeros((LANES, classes), np.float32)
    columns = np.zeros((FEAT, FEAT * PATCH), np.float32)
    meet = np.zeros((3, LANES, FEAT, PATCH), np.float32)
    for f in range(FEAT):
        columns[f, f * PATCH : (f + 1) * PATCH] = 1.0
    for k in range(classes):
        rows[k * SPAN : (k + 1) * SPAN, k] = 1.0
        rows[classes * SPAN + k, k] = 1.0
        rows[classes * (SPAN + 1) + k, k] = 1.0
        for dy in range(3):
            for i in range(PATCH):
                meet[dy, k * SPAN + i + 2 - dy, :, i] = 1.0
        meet[0, classes * SPAN + k, :, FAR_PIXEL] = 1.0
        meet[2, classes * (SPAN + 1) + k, :, NEAR_PIXEL] = 1.0
    return rows, columns, meet.reshape(3, LANES, FEAT * PATCH)


def prepare_kernel(
    up_ref, taps_ref, rows_ref, columns_ref, meet_ref, weight_ref,
    o_ref, edge_ref, held_ref, turned_ref, column_ref, sem
):
    load = pltpu.make_async_copy(weight_ref, held_ref, sem)
    load.start()
    for half in range(turned_ref.shape[0]):
        lanes = slice(128 * half, 128 * (half + 1))
        turned_ref[half] = up_ref[lanes, :].astype(f32).T
        for j in range(PATCH):
            column_ref[j, :, lanes] = turned_ref[half, pl.ds(j, FEAT * PATCH, stride=PATCH), :].astype(bf16)
    spread = []
    for dx in range(3):
        total = None
        for dy in range(3):
            taps = mm(mm(rows_ref[...], taps_ref[3 * dy + dx]).astype(bf16), columns_ref[...])
            part = taps * meet_ref[dy].astype(f32)
            total = part if total is None else total + part
        spread.append(total.astype(bf16))
    for big in range(SPAN):
        total = None
        for dx in range(3):
            j = big - 2 + dx
            if 0 <= j < PATCH:
                part = mm(spread[dx], column_ref[j])
                total = part if total is None else total + part
        o_ref[big] = total.astype(bf16)
    edge_ref[0] = mm(spread[2], column_ref[NEAR_PIXEL]).astype(bf16)
    edge_ref[1] = mm(spread[0], column_ref[FAR_PIXEL]).astype(bf16)
    load.wait()


def prepare_weights(upsample_weight, class_weight, qkv_weight):
    channels = upsample_weight.shape[0]
    tables = [jnp.asarray(table, bf16) for table in tap_tables(class_weight.shape[1])]
    whole = pl.BlockSpec(memory_space=pltpu.VMEM)
    return pl.pallas_call(
        prepare_kernel,
        in_specs=[whole] * 5 + [pl.BlockSpec(memory_space=pltpu.HBM)],
        out_specs=[whole] * 3,
        out_shape=[
            jax.ShapeDtypeStruct((SPAN, LANES, channels), bf16),
            jax.ShapeDtypeStruct((2, LANES, channels), bf16),
            pltpu.VMEM(qkv_weight.shape, bf16),
        ],
        scratch_shapes=[
            pltpu.VMEM((channels // 128, upsample_weight.shape[1], 128), f32),
            pltpu.VMEM((PATCH, FEAT * PATCH, channels), bf16),
            pltpu.SemaphoreType.DMA,
        ],
        compiler_params=pltpu.CompilerParams(vmem_limit_bytes=24 * 2**20),
        cost_estimate=pl.CostEstimate(flops=0, bytes_accessed=0, transcendentals=0),
        name="prepare_weights",
    )(upsample_weight, class_weight, *tables, pltpu.with_memory_space_constraint(qkv_weight, pltpu.HBM))


def compose_kernel(
    classes, own_ref, before_ref, after_ref, above_ref, below_ref, profile_ref, m_ref, edge_ref,
    lanes_ref, window_ref, place_ref, side_ref, bias_ref,
    o_ref, a_ref, b_ref, z_ref, z2_ref, acc_ref
):
    count = len(ENTRIES)
    edge = len(UPPER)
    own, before, after, above, below = (
        ref[...].astype(f32) for ref in (own_ref, before_ref, after_ref, above_ref, below_ref)
    )
    slot = lax.broadcasted_iota(jnp.int32, (PATCHES, LANES), 0)

    def line(tile_row, a):
        if tile_row == 1 or a is None:
            a = a if a is not None else (NEAR_PATCH if tile_row == 0 else FAR_PATCH)
            sides = [before[a : a + 1], before[PATCHES + a : PATCHES + a + 1]]
            sides += [after[a : a + 1], after[PATCHES + a : PATCHES + a + 1]]
            return own[PATCHES * a : PATCHES * (a + 1)], sides
        source = above if tile_row == 0 else below
        n = (UPPER if tile_row == 0 else LOWER).index(a)
        first = PATCHES * edge + 4 * n
        return source[PATCHES * n : PATCHES * (n + 1)], [source[first + i : first + i + 1] for i in range(4)]

    def slots(rows, base):
        for i, row in rows.items():
            base = jnp.where(slot == i, row, base)
        return base

    def second(before_row, after_row, near, far):
        rows = {i: before_row if which == 0 else after_row for i, (which, _) in enumerate(SIDE_ROWS)}
        rows[len(SIDE_ROWS)] = near
        rows[len(SIDE_ROWS) + 1] = far
        return slots(rows, jnp.zeros((SIDE, LANES), f32))

    profile = profile_ref[...].astype(f32)
    tail = slice(2 * PATCHES, 2 * PATCHES + 2)
    ends = slice((PATCHES + 4) * edge, (PATCHES + 4) * edge + 6)
    profiles = jnp.concatenate([above[ends], before[tail], profile, after[tail], below[ends]], axis=0)
    row_profiles = [profiles[2 * i : 2 * i + 1] for i in range(9)]
    col_profiles = [profiles[2 * i + 1 : 2 * i + 2] for i in range(9)]
    blank = jnp.zeros((PATCHES - 9, LANES), f32)
    row_table = jnp.concatenate(row_profiles + [blank], axis=0).astype(bf16)
    col_table = jnp.concatenate(col_profiles + [blank], axis=0).astype(bf16)
    weights = mm(row_table, lanes_ref[...])
    rows = [mm(row_table, window_ref[i]) for i in range(3)]
    cols = [mm(col_table, window_ref[i]) for i in range(3)]
    block_rows = jnp.concatenate([rows[i // 3][i : i + 1] for i in range(9)] + [blank[:, :STRIDE]], axis=0)
    block_cols = jnp.concatenate([cols[i % 3][i : i + 1] for i in range(9)] + [blank[:, :STRIDE]], axis=0)
    den = mm(block_rows.astype(bf16), block_cols.astype(bf16), TN)
    spots, side_spots = [], []
    for tile_row in range(3):
        spots.append(sum(place_ref[i].astype(f32) * block_cols[3 * tile_row + i][None] for i in range(3)).astype(bf16))
        side_spots.append(
            sum(side_ref[i].astype(f32) * block_cols[3 * tile_row + i][None] for i in range(3)).astype(bf16)
        )

    def entry_weights(n, tile_row):
        return [weights[3 * tile_row + i : 3 * tile_row + i + 1, LANES * n : LANES * (n + 1)] for i in range(3)]

    main_weights, side_weights = [], []
    for n, (tile_row, a) in enumerate(ENTRIES):
        patches, (l_far, l_near, r_near, r_far) = line(tile_row, a)
        a_ref[n] = slots({0: l_near, PATCHES - 1: r_near}, patches).astype(bf16)
        b_ref[n] = second(
            l_far, r_far, patches[NEAR_PATCH : NEAR_PATCH + 1], patches[FAR_PATCH : FAR_PATCH + 1]
        ).astype(bf16)
        left, middle, right = entry_weights(n, tile_row)
        main_weights.append(slots({0: left, PATCHES - 1: right}, jnp.broadcast_to(middle, (PATCHES, LANES))))
        side_weights.append(second(left, right, left, right))
    main_weights = jnp.stack(main_weights)
    for j in range(SPAN):
        z = mm(a_ref[...].reshape(count * PATCHES, LANES), m_ref[j], NT).reshape(count, PATCHES, LANES)
        z_ref[:, j] = (z * main_weights).astype(bf16)
    side_slot = lax.broadcasted_iota(jnp.int32, (count, SIDE, LANES), 1)
    patches = b_ref[...].astype(f32)
    total = None
    for i in range(len(SIDE_ROWS) + 2):
        kernel = m_ref[SIDE_ROWS[i][1]] if i < len(SIDE_ROWS) else edge_ref[i - len(SIDE_ROWS)]
        part = jnp.where(side_slot == i, patches, 0.0).astype(bf16).reshape(count * SIDE, LANES)
        part = mm(part, kernel, NT)
        total = part if total is None else total + part
    z2_ref[...] = (total.reshape(count, SIDE, LANES) * jnp.stack(side_weights)).astype(bf16)

    acc_ref[...] = jnp.zeros_like(acc_ref)
    for n, (tile_row, a) in enumerate(ENTRIES):
        part = mm(z_ref[n].reshape(SPAN * PATCHES, LANES), spots[tile_row], TN)
        part += mm(z2_ref[n], side_spots[tile_row], TN)
        if a is None:
            first = classes * SPAN + (classes if tile_row == 0 else 0)
            y = 2 * RIM - 1 if tile_row == 0 else STRIDE
            for k in range(classes):
                acc_ref[k, y : y + 1, :] += part[first + k : first + k + 1]
            continue
        y = PATCH * a - 1 + (tile_row - 1) * STRIDE
        low, high = 0, SPAN
        if tile_row == 0:
            high = min(SPAN, TILE_PX - (PATCH * a - 1))
        if tile_row == 2:
            low = max(0, 1 - PATCH * a)
        for k in range(classes):
            acc_ref[k, y + low : y + high, :] += part[k * SPAN + low : k * SPAN + high]
    inverse = 1.0 / jnp.maximum(den, 1.0)
    for k in range(classes):
        o_ref[k] = (acc_ref[k, RIM : RIM + STRIDE, :] + bias_ref[k] * den) * inverse


def forward(size):
    return [(i, i + 1) for i in range(size - 1)]


def backward(size):
    return [(i + 1, i) for i in range(size - 1)]


def exchange_rims(reduced, last, first, profile):
    cols = lax.axis_size("col")
    if cols == 2:
        other = swap(last, "col", 1)
        at_end = lax.axis_index("col") == 1
        before, after = jnp.where(at_end, other, 0), jnp.where(at_end, 0, other)
    else:
        before = lax.ppermute(last, "col", forward(cols))
        after = lax.ppermute(first, "col", backward(cols))

    def lines(rows):
        parts = [reduced[PATCHES * a : PATCHES * (a + 1)] for a in rows]
        for a in rows:
            for side in (before, after):
                parts += [side[a : a + 1], side[PATCHES + a : PATCHES + a + 1]]
        parts += [before[2 * PATCHES : 2 * PATCHES + 2], profile, after[2 * PATCHES : 2 * PATCHES + 2]]
        used = (PATCHES + 4) * len(rows) + 6
        parts.append(jnp.zeros((-used % 16, reduced.shape[1]), bf16))
        return jnp.concatenate(parts, axis=0)

    rows = lax.axis_size("date") * lax.axis_size("tile")
    above = lax.ppermute(lines(UPPER), ("date", "tile"), forward(rows))
    below = lax.ppermute(lines(LOWER), ("date", "tile"), backward(rows))
    return before, after, above, below


def compose(reduced, rims, profile, kernels, edges, class_bias, classes):
    channels = reduced.shape[1]
    count = len(ENTRIES)
    whole = pl.BlockSpec(memory_space=pltpu.VMEM)
    tables = [jnp.asarray(t, bf16) for t in (row_lanes(classes), windows(), PLACE_MAIN, PLACE_SIDE)]
    return pl.pallas_call(
        functools.partial(compose_kernel, classes),
        in_specs=[whole] * 12 + [pl.BlockSpec(memory_space=pltpu.SMEM)],
        out_specs=whole,
        out_shape=jax.ShapeDtypeStruct((classes, STRIDE, STRIDE), f32),
        scratch_shapes=[
            pltpu.VMEM((count, PATCHES, channels), bf16),
            pltpu.VMEM((count, SIDE, channels), bf16),
            pltpu.VMEM((count, SPAN, PATCHES, LANES), bf16),
            pltpu.VMEM((count, SIDE, LANES), bf16),
            pltpu.VMEM((classes, TILE_PX, STRIDE), f32),
        ],
        compiler_params=pltpu.CompilerParams(vmem_limit_bytes=VMEM),
        name="compose",
    )(reduced, *rims, profile, kernels, edges, *tables, class_bias.astype(f32))


def local(
    arrivals,
    owner_map,
    block_ids,
    tile_valid,
    blend_weights,
    location_table,
    norm_gain,
    qkv_weight,
    out_weight,
    final_gain,
    reduce_weight,
    reduce_bias,
    upsample_weight,
    class_weight,
    class_bias,
):
    width = arrivals.shape[-1]
    slots = arrivals.shape[1]
    classes = class_weight.shape[1]
    dates, tiles = lax.axis_size("date"), lax.axis_size("tile")
    codes = block_ids.reshape(1, 1)
    one_hot = (codes == jnp.arange(location_table.shape[0], dtype=jnp.int32)[None, :]).astype(bf16)

    def prepare(stacked):
        table, blend, up, _ = lax.optimization_barrier((location_table, blend_weights, upsample_weight, stacked))
        location = jnp.dot(one_hot, table, preferred_element_type=f32)
        profile = blend.reshape(2, TILE_PX).astype(bf16)
        profile = jnp.concatenate([profile[:1] * tile_valid.reshape(1).astype(bf16), profile[1:]], axis=0)
        profile = jnp.pad(profile, ((0, 0), (0, LANES - TILE_PX)))
        kernels, edges, held_weight = prepare_weights(up, class_weight, qkv_weight)
        return edges, location, profile, kernels, held_weight

    def use(pieces, prepared):
        return project(pieces, prepared[1], norm_gain[None], prepared[4])

    (packed, norms, x), prepared = exchange(arrivals.reshape(slots, -1, width), owner_map[0], prepare, use)
    edges, location, profile, kernels, _ = prepared
    go_last = jnp.where((lax.axis_index("col") == 0) | (lax.axis_size("col") != 2), 1, 0)
    place = jnp.stack([lax.axis_index("date"), lax.axis_index("tile"), go_last]).astype(jnp.int32)
    reduced, to_after, to_before = encode(
        place, packed, norms, x, location, out_weight, final_gain[None], reduce_weight, reduce_bias[None], profile,
        tiles, dates
    )
    rims = exchange_rims(reduced, to_after, to_before, profile)
    return compose(reduced, rims, profile, kernels, edges, class_bias, classes)[None]


def solution(mesh):
    placed = (
        P(None, None, "col", "date", "tile", None, None),
        P(),
        P(None, ("date", "tile"), "col"),
        P(None, ("date", "tile"), "col"),
        P(None, ("date", "tile"), "col", None, None),
    ) + (P(),) * 10
    return jax.shard_map(
        local,
        mesh=mesh,
        in_specs=placed,
        out_specs=P(None, None, ("date", "tile"), "col"),
        check_vma=False,
    )
```

```python
import functools
import math

import jax
import jax.numpy as jnp
import numpy as np
from jax import lax
from jax.experimental import pallas as pl
from jax.experimental.pallas import tpu as pltpu
from jax.sharding import PartitionSpec as P

HEADS = 16
DATES = 4
PATCH = 14
INTERSECTION = 32
FEAT = 16
PATCHES = 16
RIM = 16
TILE_PX = PATCH * PATCHES
STRIDE = TILE_PX - INTERSECTION
SPAN = PATCH + 2
FAR_PATCH, FAR_PIXEL = divmod(STRIDE - 1, PATCH)
NEAR_PATCH, NEAR_PIXEL = divmod(INTERSECTION, PATCH)
LANES = 256
VMEM = 56 * 2**20

EXPONENT_BOUND = 100.0
SUM_ROWS = 16
PAIR = 4
GROUP = 256

norm_eps = 1e-06
bf16 = jnp.bfloat16
f32 = jnp.float32

NN = (((1,), (0,)), ((), ()))
NT = (((1,), (1,)), ((), ()))
TN = (((0,), (0,)), ((), ()))


def mm(left, right, dims=NN):
    return lax.dot_general(left, right, dims, preferred_element_type=f32)


def layer_norm(values, gain_row):
    average = jnp.mean(values, axis=-1, keepdims=True)
    centered = values - average
    spread = jnp.mean(centered * centered, axis=-1, keepdims=True)
    return centered * lax.rsqrt(spread + norm_eps) * gain_row


def gather_kernel(dates, tiles, routes, owner_ref, a_ref, *refs):
    outs, slot_ref = refs[:-1], refs[-1]
    for slot in range(dates * tiles):
        slot_ref[owner_ref[slot]] = slot
    date, tile = lax.axis_index("date"), lax.axis_index("tile")
    for s, m, out, spot in routes:
        outs[out][spot] = a_ref[slot_ref[(date ^ m) * tiles + (tile ^ s)]]


def gather_pieces(arrivals, owner_map, groups, dates):
    slots, strip, width = arrivals.shape
    routes = [(s, m, n, i) for n, group in enumerate(groups) for i, (s, m) in enumerate(group)]
    whole = pl.BlockSpec(memory_space=pltpu.VMEM)
    return pl.pallas_call(
        functools.partial(gather_kernel, dates, slots // dates, routes),
        in_specs=[pl.BlockSpec(memory_space=pltpu.SMEM), whole],
        out_specs=[whole] * len(groups),
        out_shape=[pltpu.VMEM((len(group), strip, width), bf16) for group in groups],
        scratch_shapes=[pltpu.SMEM((slots,), jnp.int32)],
        compiler_params=pltpu.CompilerParams(vmem_limit_bytes=12 * 2**20),
        cost_estimate=pl.CostEstimate(flops=0, bytes_accessed=0, transcendentals=0),
        name="gather_pieces",
    )(owner_map, arrivals)


def swap(value, axis, mask):
    return lax.ppermute(value, axis, [(i, i ^ mask) for i in range(lax.axis_size(axis))])


def exchange(arrivals, owner_map, prepare, use):
    dates, tiles = lax.axis_size("date"), lax.axis_size("tile")
    half, late = tiles // 2, tiles - max(1, tiles // 4)
    groups = [[(s, m) for m in range(dates)] for s in range(1, late)]
    groups += [[(s, m) for s in range(late, tiles)] for m in range(dates)]
    groups += [[(0, m)] for m in range(dates)]
    pieces = gather_pieces(arrivals, owner_map, groups, dates)
    rings, mixed, own = pieces[: late - 1], pieces[late - 1 : -dates], pieces[-dates:]
    far = [swap(ring, "tile", s) for s, ring in enumerate(rings[half - 1 :], half)]
    mixed = [value if m == 0 else swap(value, "date", m) for m, value in enumerate(mixed)]
    last = [jnp.stack([value[i] for value in mixed]) for i in range(tiles - late)]
    others, last = lax.optimization_barrier((own[1:], last))
    own = [own[0]] + list(others)
    close = [swap(ring, "tile", s) for s, ring in enumerate(rings[: half - 1], 1)]
    own = [value if m == 0 else swap(value, "date", m) for m, value in enumerate(own)]
    prepared = prepare(last)
    far, last, first = lax.optimization_barrier((far, last, prepared[0]))
    prepared = (first,) + prepared[1:]
    last = [(swap(pieces, "tile", s), None) for s, pieces in enumerate(last, late)]

    def cross_dates(ring):
        return [(ring if m == 0 else swap(ring[m : m + 1], "date", m), 0) for m in range(dates)]

    near = [(value, 0) for value in own]
    for ring in close:
        near += cross_dates(ring)
    middle = []
    for ring in far:
        middle += cross_dates(ring)
    return zip(*[use(pieces, prepared) for pieces in (near, middle, last)]), prepared


def with_ones(values):
    return jnp.concatenate([values, jnp.ones((SUM_ROWS, values.shape[1]), bf16)], axis=0)


def normalize(x, loc_ref, gain_ref):
    return layer_norm(x.astype(f32) + loc_ref[...], gain_ref[...].astype(f32)).astype(bf16)


def project_block(weight_ref, normed, packed_ref, norm_ref):
    width = weight_ref.shape[0]
    block = width // 2
    heads = HEADS // 2
    for first in range(0, weight_ref.shape[1], block):
        packed = mm(weight_ref[:, first : first + block], normed, (((0,), (1,)), ((), ()))).astype(bf16)
        packed_ref[first : first + block, :] = packed
        if first < 2 * width:
            packed = packed.astype(f32)
            squares = jnp.sum((packed * packed).reshape(heads, block // heads, packed.shape[1]), axis=1)
            largest = jnp.max(squares, axis=1, keepdims=True)
            row = first // block * heads
            norm_ref[row : row + heads, :] = jnp.broadcast_to(largest, (heads, norm_ref.shape[1]))


def project_kernel(places, *refs):
    count = len(places)
    piece_refs, (loc_ref, gain_ref, weight_ref, packed_ref, norm_ref, x_ref, normed_ref) = refs[:count], refs[count:]
    first = 0
    for piece_ref, place in zip(piece_refs, places):
        x = piece_ref[...].reshape(-1, piece_ref.shape[-1]) if place is None else piece_ref[place]
        x_ref[first : first + x.shape[0], :] = x
        normed_ref[first : first + x.shape[0], :] = normalize(x, loc_ref, gain_ref)
        first += x.shape[0]
    project_block(weight_ref, normed_ref[...], packed_ref, norm_ref)


def project(pieces, location, gain, weight):
    width = weight.shape[0]
    tokens = sum(piece.shape[1] * (piece.shape[0] if n is None else 1) for piece, n in pieces)
    whole = pl.BlockSpec(memory_space=pltpu.VMEM)
    specs = [
        pl.BlockSpec(piece.shape if n is None else (1,) + piece.shape[1:], lambda i: (0, 0, 0)) for piece, n in pieces
    ]
    return pl.pallas_call(
        functools.partial(project_kernel, [n for _, n in pieces]),
        grid=(1,),
        in_specs=specs + [whole] * 3,
        out_specs=[whole] * 3,
        out_shape=[
            jax.ShapeDtypeStruct((weight.shape[1], tokens), bf16),
            jax.ShapeDtypeStruct((2 * HEADS, 128), f32),
            jax.ShapeDtypeStruct((tokens, width), bf16),
        ],
        scratch_shapes=[pltpu.VMEM((tokens, width), bf16)],
        compiler_params=pltpu.CompilerParams(vmem_limit_bytes=16 * 2**20),
        cost_estimate=pl.CostEstimate(flops=0, bytes_accessed=0, transcendentals=0),
        name="project",
    )(*[piece for piece, _ in pieces], location, gain, weight)


def encode_kernel(parts, place_ref, *refs):
    packed_refs, norm_refs, x_refs = (refs[i * parts : (i + 1) * parts] for i in range(3))
    (
        loc_ref, out_ref, final_ref, wr_ref, bias_ref, profile_ref,
        o_ref, last_ref, first_ref, mixed_ref, encoded_ref, reduced_ref
    ) = refs[3 * parts :]
    width = out_ref.shape[0]
    head = width // HEADS
    scale = math.log2(math.e) / math.sqrt(head)
    norms = norm_refs[0][...]
    for norm_ref in norm_refs[1:]:
        norms = jnp.maximum(norms, norm_ref[...])
    small = jnp.max(norms[:HEADS] * norms[HEADS:]) <= (EXPONENT_BOUND / scale) ** 2

    def side_by_side(which, n):
        rows = pl.ds(pl.multiple_of(which * width + n * head, 16), head)
        return jnp.concatenate([ref[rows, :] for ref in packed_refs], axis=1)

    def scores(n):
        return mm(side_by_side(1, n), side_by_side(0, n), TN)

    def finish(n, lifted):
        sums = mm(with_ones(side_by_side(2, n)), lifted.astype(bf16))
        rows = pl.ds(pl.multiple_of(n * head, 16), head)
        mixed_ref[rows, :] = (sums[:head] * (1.0 / sums[head : head + 1])).astype(bf16)

    @pl.when(small)
    def _():
        def heads(pair, carry):
            for n in range(PAIR):
                finish(pair * PAIR + n, jnp.exp2(scores(pair * PAIR + n) * scale))
            return carry

        lax.fori_loop(0, HEADS // PAIR, heads, 0)

    @pl.when(jnp.logical_not(small))
    def _():
        def heads(n, carry):
            held = scores(n)
            finish(n, jnp.exp2((held - jnp.max(held, axis=0, keepdims=True)) * scale))
            return carry

        lax.fori_loop(0, HEADS, heads, 0)

    tiles, dates, strip, _ = encoded_ref.shape
    first = 0
    step = tiles * dates * strip // 4
    for held_ref in x_refs:
        for row in range(0, held_ref.shape[0], step):
            held = held_ref[row : row + step, :].astype(f32) + loc_ref[...]
            updated = held + mm(mixed_ref[:, first : first + step], out_ref[...], TN)
            encoded = layer_norm(updated, final_ref[...].astype(f32)).astype(bf16)
            part = step // (dates * strip)
            group = first // (dates * strip)
            encoded_ref[group : group + part] = encoded.reshape(part, dates, strip, width)
            first += step
    total = bias_ref[...].astype(f32)
    for m in range(dates):
        total = total + mm(encoded_ref[:, m].reshape(tiles * strip, width), wr_ref[place_ref[0] ^ m])
    total = 0.5 * total * (1.0 + lax.erf(total * math.sqrt(0.5)))
    halves = range(reduced_ref.shape[0])
    for s in range(tiles):
        spot = pl.multiple_of((place_ref[1] ^ s) * strip, strip)
        for half in halves:
            lanes = slice(128 * half, 128 * (half + 1))
            reduced_ref[half, pl.ds(spot, strip), :] = total[s * strip : (s + 1) * strip, lanes]
    for half in halves:
        o_ref[:, 128 * half : 128 * (half + 1)] = reduced_ref[half].astype(bf16)

    def column(b):
        return jnp.concatenate([reduced_ref[half, pl.ds(b, PATCHES, stride=PATCHES), :] for half in halves], axis=1)

    tail = jnp.zeros((PATCHES - 2, o_ref.shape[1]), f32)
    tail = jnp.concatenate([profile_ref[...].astype(f32), tail], axis=0)
    is_last = place_ref[2] == 1
    sent = [jnp.where(is_last, column(PATCHES - 2 + i), column(i)) for i in range(2)]
    last_ref[...] = jnp.concatenate(sent + [tail], axis=0).astype(bf16)
    first_ref[...] = jnp.concatenate([column(0), column(1), tail], axis=0).astype(bf16)


def encode(
    place, packed, norms, x, location, out_weight, final_gain, reduce_weight, reduce_bias, profile, tiles, dates
):
    width = out_weight.shape[0]
    tokens = sum(part.shape[0] for part in x)
    strip = tokens // (tiles * dates)
    dec = reduce_weight.shape[1]
    patches = tiles * strip
    sent = jax.ShapeDtypeStruct((3 * PATCHES, dec), bf16)
    whole = pl.BlockSpec(memory_space=pltpu.VMEM)
    return pl.pallas_call(
        functools.partial(encode_kernel, len(packed)),
        in_specs=[pl.BlockSpec(memory_space=pltpu.SMEM)] + [whole] * (3 * len(packed) + 6),
        out_specs=[whole] * 3,
        out_shape=[jax.ShapeDtypeStruct((patches, dec), bf16), sent, sent],
        scratch_shapes=[
            pltpu.VMEM((width, tokens), bf16),
            pltpu.VMEM((tiles, dates, strip, width), bf16),
            pltpu.VMEM((dec // 128, patches, 128), f32),
        ],
        compiler_params=pltpu.CompilerParams(vmem_limit_bytes=28 * 2**20),
        name="encode",
    )(
        place, *packed, *norms, *x, location, out_weight, final_gain,
        reduce_weight.reshape(dates, width, dec), reduce_bias, profile,
    )


FIRST_OWN = RIM // PATCH
LAST_OWN = PATCHES - 1 - FIRST_OWN
UPPER = [a for a in range(PATCHES) if PATCH * a + PATCH >= TILE_PX - RIM]
LOWER = [a for a in range(PATCHES) if PATCH * a - 1 < RIM]
ENTRIES = (
    [(0, a) for a in UPPER]
    + [(0, None)]
    + [(1, a) for a in range(FIRST_OWN, LAST_OWN + 1)]
    + [(2, a) for a in LOWER]
    + [(2, None)]
)
SIDE = 16


def placement():
    main = np.zeros((3, SPAN, PATCHES, STRIDE), np.float32)
    side = np.zeros((3, SIDE, STRIDE), np.float32)
    for j in range(SPAN):
        for slot in range(PATCHES):
            if slot == 0:
                which, x = 0, PATCH * (PATCHES - 1) + j - 1
            elif slot == PATCHES - 1:
                which, x = 2, j - 1
            else:
                which, x = 1, PATCH * slot + j - 1
            column = x + (which - 1) * STRIDE - RIM
            if 0 <= x < TILE_PX and 0 <= column < STRIDE:
                main[which, j, slot, column] = 1.0
    rows = []
    for j in range(SPAN):
        x = PATCH * (PATCHES - 2) + j - 1
        if TILE_PX - RIM <= x < TILE_PX:
            side[0, len(rows), x - (TILE_PX - RIM)] = 1.0
            rows.append((0, j))
    for j in range(SPAN):
        x = PATCH + j - 1
        if 0 <= x < RIM:
            side[2, len(rows), STRIDE - RIM + x] = 1.0
            rows.append((2, j))
    side[0, len(rows), RIM - 1] = 1.0
    side[2, len(rows) + 1, STRIDE - RIM] = 1.0
    return main.reshape(3, SPAN * PATCHES, STRIDE), side, rows


PLACE_MAIN, PLACE_SIDE, SIDE_ROWS = placement()


def windows():
    table = np.zeros((3, LANES, STRIDE), np.float32)
    for x in range(STRIDE):
        table[1, x + RIM, x] = 1.0
    for x in range(RIM):
        table[0, TILE_PX - RIM + x, x] = 1.0
        table[2, x, STRIDE - RIM + x] = 1.0
    return table


def row_lanes(classes):
    table = np.zeros((LANES, len(ENTRIES), LANES), np.float32)
    for n, (tile_row, a) in enumerate(ENTRIES):
        for k in range(classes):
            if a is None:
                halo = classes * SPAN + k + (classes if tile_row == 0 else 0)
                table[TILE_PX - 1 if tile_row == 0 else 0, n, halo] = 1.0
                continue
            for i in range(SPAN):
                y = PATCH * a - 1 + i
                if 0 <= y < TILE_PX:
                    table[y, n, k * SPAN + i] = 1.0
    return table.reshape(LANES, -1)


def tap_tables(classes):
    rows = np.zeros((LANES, classes), np.float32)
    columns = np.zeros((FEAT, FEAT * PATCH), np.float32)
    meet = np.zeros((3, LANES, FEAT, PATCH), np.float32)
    for f in range(FEAT):
        columns[f, f * PATCH : (f + 1) * PATCH] = 1.0
    for k in range(classes):
        rows[k * SPAN : (k + 1) * SPAN, k] = 1.0
        rows[classes * SPAN + k, k] = 1.0
        rows[classes * (SPAN + 1) + k, k] = 1.0
        for dy in range(3):
            for i in range(PATCH):
                meet[dy, k * SPAN + i + 2 - dy, :, i] = 1.0
        meet[0, classes * SPAN + k, :, FAR_PIXEL] = 1.0
        meet[2, classes * (SPAN + 1) + k, :, NEAR_PIXEL] = 1.0
    return rows, columns, meet.reshape(3, LANES, FEAT * PATCH)


def prepare_kernel(
    up_ref, taps_ref, rows_ref, columns_ref, meet_ref, weight_ref,
    o_ref, edge_ref, held_ref, turned_ref, column_ref, sem
):
    load = pltpu.make_async_copy(weight_ref, held_ref, sem)
    load.start()
    for half in range(turned_ref.shape[0]):
        lanes = slice(128 * half, 128 * (half + 1))
        turned_ref[half] = up_ref[lanes, :].astype(f32).T
        for j in range(PATCH):
            column_ref[j, :, lanes] = turned_ref[half, pl.ds(j, FEAT * PATCH, stride=PATCH), :].astype(bf16)
    spread = []
    for dx in range(3):
        total = None
        for dy in range(3):
            taps = mm(mm(rows_ref[...], taps_ref[3 * dy + dx]).astype(bf16), columns_ref[...])
            part = taps * meet_ref[dy].astype(f32)
            total = part if total is None else total + part
        spread.append(total.astype(bf16))
    for big in range(SPAN):
        total = None
        for dx in range(3):
            j = big - 2 + dx
            if 0 <= j < PATCH:
                part = mm(spread[dx], column_ref[j])
                total = part if total is None else total + part
        o_ref[big] = total.astype(bf16)
    edge_ref[0] = mm(spread[2], column_ref[NEAR_PIXEL]).astype(bf16)
    edge_ref[1] = mm(spread[0], column_ref[FAR_PIXEL]).astype(bf16)
    load.wait()


def prepare_weights(upsample_weight, class_weight, qkv_weight):
    channels = upsample_weight.shape[0]
    tables = [jnp.asarray(table, bf16) for table in tap_tables(class_weight.shape[1])]
    whole = pl.BlockSpec(memory_space=pltpu.VMEM)
    return pl.pallas_call(
        prepare_kernel,
        in_specs=[whole] * 5 + [pl.BlockSpec(memory_space=pltpu.HBM)],
        out_specs=[whole] * 3,
        out_shape=[
            jax.ShapeDtypeStruct((SPAN, LANES, channels), bf16),
            jax.ShapeDtypeStruct((2, LANES, channels), bf16),
            pltpu.VMEM(qkv_weight.shape, bf16),
        ],
        scratch_shapes=[
            pltpu.VMEM((channels // 128, upsample_weight.shape[1], 128), f32),
            pltpu.VMEM((PATCH, FEAT * PATCH, channels), bf16),
            pltpu.SemaphoreType.DMA,
        ],
        compiler_params=pltpu.CompilerParams(vmem_limit_bytes=24 * 2**20),
        cost_estimate=pl.CostEstimate(flops=0, bytes_accessed=0, transcendentals=0),
        name="prepare_weights",
    )(upsample_weight, class_weight, *tables, pltpu.with_memory_space_constraint(qkv_weight, pltpu.HBM))


def compose_kernel(
    classes, own_ref, before_ref, after_ref, above_ref, below_ref, profile_ref, m_ref, edge_ref,
    lanes_ref, window_ref, place_ref, side_ref, bias_ref,
    o_ref, a_ref, b_ref, z_ref, z2_ref, acc_ref, out_ref, sems
):
    count = len(ENTRIES)
    edge = len(UPPER)
    own, before, after, above, below = (
        ref[...].astype(f32) for ref in (own_ref, before_ref, after_ref, above_ref, below_ref)
    )
    slot = lax.broadcasted_iota(jnp.int32, (PATCHES, LANES), 0)

    def line(tile_row, a):
        if tile_row == 1 or a is None:
            a = a if a is not None else (NEAR_PATCH if tile_row == 0 else FAR_PATCH)
            sides = [before[a : a + 1], before[PATCHES + a : PATCHES + a + 1]]
            sides += [after[a : a + 1], after[PATCHES + a : PATCHES + a + 1]]
            return own[PATCHES * a : PATCHES * (a + 1)], sides
        source = above if tile_row == 0 else below
        n = (UPPER if tile_row == 0 else LOWER).index(a)
        first = PATCHES * edge + 4 * n
        return source[PATCHES * n : PATCHES * (n + 1)], [source[first + i : first + i + 1] for i in range(4)]

    def slots(rows, base):
        for i, row in rows.items():
            base = jnp.where(slot == i, row, base)
        return base

    def second(before_row, after_row, near, far):
        rows = {i: before_row if which == 0 else after_row for i, (which, _) in enumerate(SIDE_ROWS)}
        rows[len(SIDE_ROWS)] = near
        rows[len(SIDE_ROWS) + 1] = far
        return slots(rows, jnp.zeros((SIDE, LANES), f32))

    profile = profile_ref[...].astype(f32)
    tail = slice(2 * PATCHES, 2 * PATCHES + 2)
    ends = slice((PATCHES + 4) * edge, (PATCHES + 4) * edge + 6)
    profiles = jnp.concatenate([above[ends], before[tail], profile, after[tail], below[ends]], axis=0)
    row_profiles = [profiles[2 * i : 2 * i + 1] for i in range(9)]
    col_profiles = [profiles[2 * i + 1 : 2 * i + 2] for i in range(9)]
    blank = jnp.zeros((PATCHES - 9, LANES), f32)
    row_table = jnp.concatenate(row_profiles + [blank], axis=0).astype(bf16)
    col_table = jnp.concatenate(col_profiles + [blank], axis=0).astype(bf16)
    weights = mm(row_table, lanes_ref[...])
    rows = [mm(row_table, window_ref[i]) for i in range(3)]
    cols = [mm(col_table, window_ref[i]) for i in range(3)]
    block_rows = jnp.concatenate([rows[i // 3][i : i + 1] for i in range(9)] + [blank[:, :STRIDE]], axis=0)
    block_cols = jnp.concatenate([cols[i % 3][i : i + 1] for i in range(9)] + [blank[:, :STRIDE]], axis=0)
    den = mm(block_rows.astype(bf16), block_cols.astype(bf16), TN)
    spots, side_spots = [], []
    for tile_row in range(3):
        spots.append(sum(place_ref[i].astype(f32) * block_cols[3 * tile_row + i][None] for i in range(3)).astype(bf16))
        side_spots.append(
            sum(side_ref[i].astype(f32) * block_cols[3 * tile_row + i][None] for i in range(3)).astype(bf16)
        )

    def entry_weights(n, tile_row):
        return [weights[3 * tile_row + i : 3 * tile_row + i + 1, LANES * n : LANES * (n + 1)] for i in range(3)]

    main_weights, side_weights = [], []
    for n, (tile_row, a) in enumerate(ENTRIES):
        patches, (l_far, l_near, r_near, r_far) = line(tile_row, a)
        a_ref[n] = slots({0: l_near, PATCHES - 1: r_near}, patches).astype(bf16)
        b_ref[n] = second(
            l_far, r_far, patches[NEAR_PATCH : NEAR_PATCH + 1], patches[FAR_PATCH : FAR_PATCH + 1]
        ).astype(bf16)
        left, middle, right = entry_weights(n, tile_row)
        main_weights.append(slots({0: left, PATCHES - 1: right}, jnp.broadcast_to(middle, (PATCHES, LANES))))
        side_weights.append(second(left, right, left, right))
    main_weights = jnp.stack(main_weights)
    for j in range(SPAN):
        z = mm(a_ref[...].reshape(count * PATCHES, LANES), m_ref[j], NT).reshape(count, PATCHES, LANES)
        z_ref[:, j] = (z * main_weights).astype(bf16)
    side_slot = lax.broadcasted_iota(jnp.int32, (count, SIDE, LANES), 1)
    patches = b_ref[...].astype(f32)
    total = None
    for i in range(len(SIDE_ROWS) + 2):
        kernel = m_ref[SIDE_ROWS[i][1]] if i < len(SIDE_ROWS) else edge_ref[i - len(SIDE_ROWS)]
        part = jnp.where(side_slot == i, patches, 0.0).astype(bf16).reshape(count * SIDE, LANES)
        part = mm(part, kernel, NT)
        total = part if total is None else total + part
    z2_ref[...] = (total.reshape(count, SIDE, LANES) * jnp.stack(side_weights)).astype(bf16)

    acc_ref[...] = jnp.zeros_like(acc_ref)
    inverse = 1.0 / jnp.maximum(den, 1.0)
    step = STRIDE // sems.shape[0]
    copies = []

    def finish():
        first = len(copies) * step
        rows = slice(first, first + step)
        for k in range(classes):
            total = acc_ref[k, RIM + first : RIM + first + step, :] + bias_ref[k] * den[rows]
            out_ref[k, rows, :] = total * inverse[rows]
        copies.append(pltpu.make_async_copy(out_ref.at[:, rows, :], o_ref.at[:, rows, :], sems.at[len(copies)]))
        copies[-1].start()

    for n, (tile_row, a) in enumerate(ENTRIES):
        part = mm(z_ref[n].reshape(SPAN * PATCHES, LANES), spots[tile_row], TN)
        part += mm(z2_ref[n], side_spots[tile_row], TN)
        if a is None:
            first = classes * SPAN + (classes if tile_row == 0 else 0)
            y = 2 * RIM - 1 if tile_row == 0 else STRIDE
            for k in range(classes):
                acc_ref[k, y : y + 1, :] += part[first + k : first + k + 1]
            continue
        y = PATCH * a - 1 + (tile_row - 1) * STRIDE
        low, high = 0, SPAN
        if tile_row == 0:
            high = min(SPAN, TILE_PX - (PATCH * a - 1))
        if tile_row == 2:
            low = max(0, 1 - PATCH * a)
        for k in range(classes):
            acc_ref[k, y + low : y + high, :] += part[k * SPAN + low : k * SPAN + high]
        if tile_row == 1:
            clear = min(y + PATCH, STRIDE) - RIM
            while (len(copies) + 1) * step <= clear and len(copies) + 1 < sems.shape[0]:
                finish()
    while len(copies) < sems.shape[0]:
        finish()
    for copy in copies:
        copy.wait()


def forward(size):
    return [(i, i + 1) for i in range(size - 1)]


def backward(size):
    return [(i + 1, i) for i in range(size - 1)]


def forward(size):
    return [(i, i + 1) for i in range(size - 1)]


def backward(size):
    return [(i + 1, i) for i in range(size - 1)]


def exchange_rims(reduced, last, first, profile):
    cols = lax.axis_size("col")
    if cols == 2:
        other = swap(last, "col", 1)
        at_end = lax.axis_index("col") == 1
        before, after = jnp.where(at_end, other, 0), jnp.where(at_end, 0, other)
    else:
        before = lax.ppermute(last, "col", forward(cols))
        after = lax.ppermute(first, "col", backward(cols))

    def lines(rows):
        parts = [reduced[PATCHES * a : PATCHES * (a + 1)] for a in rows]
        for a in rows:
            for side in (before, after):
                parts += [side[a : a + 1], side[PATCHES + a : PATCHES + a + 1]]
        parts += [before[2 * PATCHES : 2 * PATCHES + 2], profile, after[2 * PATCHES : 2 * PATCHES + 2]]
        used = (PATCHES + 4) * len(rows) + 6
        parts.append(jnp.zeros((-used % 16, reduced.shape[1]), bf16))
        return jnp.concatenate(parts, axis=0)

    rows = lax.axis_size("date") * lax.axis_size("tile")
    above = lax.ppermute(lines(UPPER), ("date", "tile"), forward(rows))
    below = lax.ppermute(lines(LOWER), ("date", "tile"), backward(rows))
    return before, after, above, below


def compose(reduced, rims, profile, kernels, edges, class_bias, classes):
    channels = reduced.shape[1]
    count = len(ENTRIES)
    whole = pl.BlockSpec(memory_space=pltpu.VMEM)
    tables = [jnp.asarray(t, bf16) for t in (row_lanes(classes), windows(), PLACE_MAIN, PLACE_SIDE)]
    return pl.pallas_call(
        functools.partial(compose_kernel, classes),
        in_specs=[whole] * 12 + [pl.BlockSpec(memory_space=pltpu.SMEM)],
        out_specs=pl.BlockSpec(memory_space=pl.ANY),
        out_shape=jax.ShapeDtypeStruct((classes, STRIDE, STRIDE), f32),
        scratch_shapes=[
            pltpu.VMEM((count, PATCHES, channels), bf16),
            pltpu.VMEM((count, SIDE, channels), bf16),
            pltpu.VMEM((count, SPAN, PATCHES, LANES), bf16),
            pltpu.VMEM((count, SIDE, LANES), bf16),
            pltpu.VMEM((classes, TILE_PX, STRIDE), f32),
            pltpu.VMEM((classes, STRIDE, STRIDE), f32),
            pltpu.SemaphoreType.DMA((4,)),
        ],
        compiler_params=pltpu.CompilerParams(vmem_limit_bytes=52 * 2**20),
        name="compose",
    )(reduced, *rims, profile, kernels, edges, *tables, class_bias.astype(f32))


def local(
    arrivals,
    owner_map,
    block_ids,
    tile_valid,
    blend_weights,
    location_table,
    norm_gain,
    qkv_weight,
    out_weight,
    final_gain,
    reduce_weight,
    reduce_bias,
    upsample_weight,
    class_weight,
    class_bias,
):
    width = arrivals.shape[-1]
    slots = arrivals.shape[1]
    classes = class_weight.shape[1]
    dates, tiles = lax.axis_size("date"), lax.axis_size("tile")
    codes = block_ids.reshape(1, 1)
    one_hot = (codes == jnp.arange(location_table.shape[0], dtype=jnp.int32)[None, :]).astype(bf16)

    def prepare(stacked):
        table, blend, up, _ = lax.optimization_barrier((location_table, blend_weights, upsample_weight, stacked))
        location = jnp.dot(one_hot, table, preferred_element_type=f32)
        profile = blend.reshape(2, TILE_PX).astype(bf16)
        profile = jnp.concatenate([profile[:1] * tile_valid.reshape(1).astype(bf16), profile[1:]], axis=0)
        profile = jnp.pad(profile, ((0, 0), (0, LANES - TILE_PX)))
        kernels, edges, held_weight = prepare_weights(up, class_weight, qkv_weight)
        return edges, location, profile, kernels, held_weight

    def use(pieces, prepared):
        return project(pieces, prepared[1], norm_gain[None], prepared[4])

    (packed, norms, x), prepared = exchange(arrivals.reshape(slots, -1, width), owner_map[0], prepare, use)
    edges, location, profile, kernels, _ = prepared
    go_last = jnp.where((lax.axis_index("col") == 0) | (lax.axis_size("col") != 2), 1, 0)
    place = jnp.stack([lax.axis_index("date"), lax.axis_index("tile"), go_last]).astype(jnp.int32)
    reduced, to_after, to_before = encode(
        place, packed, norms, x, location, out_weight, final_gain[None], reduce_weight, reduce_bias[None], profile,
        tiles, dates
    )
    rims = exchange_rims(reduced, to_after, to_before, profile)
    return compose(reduced, rims, profile, kernels, edges, class_bias, classes)[None]


def solution(mesh):
    placed = (
        P(None, None, "col", "date", "tile", None, None),
        P(),
        P(None, ("date", "tile"), "col"),
        P(None, ("date", "tile"), "col"),
        P(None, ("date", "tile"), "col", None, None),
    ) + (P(),) * 10
    return jax.shard_map(
        local,
        mesh=mesh,
        in_specs=placed,
        out_specs=P(None, None, ("date", "tile"), "col"),
        check_vma=False,
    )
```

```python
import functools
import math

import jax
import jax.numpy as jnp
import numpy as np
from jax import lax
from jax.experimental import pallas as pl
from jax.experimental.pallas import tpu as pltpu
from jax.sharding import PartitionSpec as P

HEADS = 16
DATES = 4
PATCH = 14
INTERSECTION = 32
FEAT = 16
PATCHES = 16
RIM = 16
TILE_PX = PATCH * PATCHES
STRIDE = TILE_PX - INTERSECTION
SPAN = PATCH + 2
FAR_PATCH, FAR_PIXEL = divmod(STRIDE - 1, PATCH)
NEAR_PATCH, NEAR_PIXEL = divmod(INTERSECTION, PATCH)
LANES = 256
VMEM = 56 * 2**20

EXPONENT_BOUND = 100.0
SUM_ROWS = 16
PAIR = 8
GROUP = 256

norm_eps = 1e-06
bf16 = jnp.bfloat16
f32 = jnp.float32

NN = (((1,), (0,)), ((), ()))
NT = (((1,), (1,)), ((), ()))
TN = (((0,), (0,)), ((), ()))


def mm(left, right, dims=NN):
    return lax.dot_general(left, right, dims, preferred_element_type=f32)


def layer_norm(values, gain_row):
    average = jnp.mean(values, axis=-1, keepdims=True)
    centered = values - average
    spread = jnp.mean(centered * centered, axis=-1, keepdims=True)
    return centered * lax.rsqrt(spread + norm_eps) * gain_row


def gather_kernel(dates, tiles, routes, owner_ref, a_ref, *refs):
    outs, slot_ref = refs[:-1], refs[-1]
    for slot in range(dates * tiles):
        slot_ref[owner_ref[slot]] = slot
    date, tile = lax.axis_index("date"), lax.axis_index("tile")
    for s, m, out, spot in routes:
        outs[out][spot] = a_ref[slot_ref[(date ^ m) * tiles + (tile ^ s)]]


def gather_pieces(arrivals, owner_map, groups, dates):
    slots, strip, width = arrivals.shape
    routes = [(s, m, n, i) for n, group in enumerate(groups) for i, (s, m) in enumerate(group)]
    whole = pl.BlockSpec(memory_space=pltpu.VMEM)
    return pl.pallas_call(
        functools.partial(gather_kernel, dates, slots // dates, routes),
        in_specs=[pl.BlockSpec(memory_space=pltpu.SMEM), whole],
        out_specs=[whole] * len(groups),
        out_shape=[jax.ShapeDtypeStruct((len(group), strip, width), bf16) for group in groups],
        scratch_shapes=[pltpu.SMEM((slots,), jnp.int32)],
        compiler_params=pltpu.CompilerParams(vmem_limit_bytes=12 * 2**20),
        cost_estimate=pl.CostEstimate(flops=0, bytes_accessed=0, transcendentals=0),
        name="gather_pieces",
    )(owner_map, arrivals)


def swap(value, axis, mask):
    return lax.ppermute(value, axis, [(i, i ^ mask) for i in range(lax.axis_size(axis))])


def exchange(arrivals, owner_map, prepare, use):
    dates, tiles = lax.axis_size("date"), lax.axis_size("tile")
    half, late = tiles // 2, tiles - max(1, tiles // 4)
    groups = [[(s, m) for m in range(dates)] for s in range(1, late)]
    groups += [[(s, m) for s in range(late, tiles)] for m in range(dates)]
    groups += [[(0, m)] for m in range(dates)]
    pieces = gather_pieces(arrivals, owner_map, groups, dates)
    rings, mixed, own = pieces[: late - 1], pieces[late - 1 : -dates], pieces[-dates:]
    far = [swap(ring, "tile", s) for s, ring in enumerate(rings[half - 1 :], half)]
    mixed = [value if m == 0 else swap(value, "date", m) for m, value in enumerate(mixed)]
    last = [jnp.stack([value[i] for value in mixed]) for i in range(tiles - late)]
    others, last = lax.optimization_barrier((own[1:], last))
    own = [own[0]] + list(others)
    close = [swap(ring, "tile", s) for s, ring in enumerate(rings[: half - 1], 1)]
    own = [value if m == 0 else swap(value, "date", m) for m, value in enumerate(own)]
    prepared = prepare(last)
    far, last, first = lax.optimization_barrier((far, last, prepared[0]))
    prepared = (first,) + prepared[1:]
    last = [(swap(pieces, "tile", s), None) for s, pieces in enumerate(last, late)]

    def cross_dates(ring):
        return [(ring if m == 0 else swap(ring[m : m + 1], "date", m), 0) for m in range(dates)]

    near = [(value, 0) for value in own]
    for ring in close:
        near += cross_dates(ring)
    middle = []
    for ring in far:
        middle += cross_dates(ring)
    return zip(*[use(pieces, prepared) for pieces in (near, middle, last)]), prepared


def with_ones(values):
    return jnp.concatenate([values, jnp.ones((SUM_ROWS, values.shape[1]), bf16)], axis=0)


def normalize(x, loc_ref, gain_ref):
    return layer_norm(x.astype(f32) + loc_ref[...], gain_ref[...].astype(f32)).astype(bf16)


def project_block(weight_ref, normed, packed_ref, norm_ref):
    width = weight_ref.shape[0]
    block = width // 2
    heads = HEADS // 2
    for first in range(0, weight_ref.shape[1], block):
        packed = mm(weight_ref[:, first : first + block], normed, (((0,), (1,)), ((), ()))).astype(bf16)
        packed_ref[first : first + block, :] = packed
        if first < 2 * width:
            packed = packed.astype(f32)
            squares = jnp.sum((packed * packed).reshape(heads, block // heads, packed.shape[1]), axis=1)
            largest = jnp.max(squares, axis=1, keepdims=True)
            row = first // block * heads
            norm_ref[row : row + heads, :] = jnp.broadcast_to(largest, (heads, norm_ref.shape[1]))


def project_kernel(places, *refs):
    count = len(places)
    piece_refs, (loc_ref, gain_ref, weight_ref, packed_ref, norm_ref, x_ref, normed_ref) = refs[:count], refs[count:]
    first = 0
    for piece_ref, place in zip(piece_refs, places):
        x = piece_ref[...].reshape(-1, piece_ref.shape[-1]) if place is None else piece_ref[place]
        x_ref[first : first + x.shape[0], :] = x
        normed_ref[first : first + x.shape[0], :] = normalize(x, loc_ref, gain_ref)
        first += x.shape[0]
    project_block(weight_ref, normed_ref[...], packed_ref, norm_ref)


def project(pieces, location, gain, weight):
    width = weight.shape[0]
    tokens = sum(piece.shape[1] * (piece.shape[0] if n is None else 1) for piece, n in pieces)
    whole = pl.BlockSpec(memory_space=pltpu.VMEM)
    specs = [
        pl.BlockSpec(piece.shape if n is None else (1,) + piece.shape[1:], lambda i: (0, 0, 0)) for piece, n in pieces
    ]
    return pl.pallas_call(
        functools.partial(project_kernel, [n for _, n in pieces]),
        grid=(1,),
        in_specs=specs + [whole] * 3,
        out_specs=[whole] * 3,
        out_shape=[
            jax.ShapeDtypeStruct((weight.shape[1], tokens), bf16),
            jax.ShapeDtypeStruct((2 * HEADS, 128), f32),
            jax.ShapeDtypeStruct((tokens, width), bf16),
        ],
        scratch_shapes=[pltpu.VMEM((tokens, width), bf16)],
        compiler_params=pltpu.CompilerParams(vmem_limit_bytes=16 * 2**20),
        cost_estimate=pl.CostEstimate(flops=0, bytes_accessed=0, transcendentals=0),
        name="project",
    )(*[piece for piece, _ in pieces], location, gain, weight)


def encode_kernel(parts, place_ref, *refs):
    packed_refs, norm_refs, x_refs = (refs[i * parts : (i + 1) * parts] for i in range(3))
    (
        loc_ref, out_ref, final_ref, wr_ref, bias_ref, profile_ref,
        o_ref, last_ref, first_ref, mixed_ref, encoded_ref, reduced_ref
    ) = refs[3 * parts :]
    width = out_ref.shape[0]
    head = width // HEADS
    scale = math.log2(math.e) / math.sqrt(head)
    norms = norm_refs[0][...]
    for norm_ref in norm_refs[1:]:
        norms = jnp.maximum(norms, norm_ref[...])
    small = jnp.max(norms[:HEADS] * norms[HEADS:]) <= (EXPONENT_BOUND / scale) ** 2

    def side_by_side(which, n):
        rows = pl.ds(pl.multiple_of(which * width + n * head, 16), head)
        return jnp.concatenate([ref[rows, :] for ref in packed_refs], axis=1)

    def scores(n):
        return mm(side_by_side(1, n), side_by_side(0, n), TN)

    def finish(n, lifted):
        sums = mm(with_ones(side_by_side(2, n)), lifted.astype(bf16))
        rows = pl.ds(pl.multiple_of(n * head, 16), head)
        mixed_ref[rows, :] = (sums[:head] * (1.0 / sums[head : head + 1])).astype(bf16)

    @pl.when(small)
    def _():
        def heads(pair, carry):
            for n in range(PAIR):
                finish(pair * PAIR + n, jnp.exp2(scores(pair * PAIR + n) * scale))
            return carry

        lax.fori_loop(0, HEADS // PAIR, heads, 0)

    @pl.when(jnp.logical_not(small))
    def _():
        def heads(n, carry):
            held = scores(n)
            finish(n, jnp.exp2((held - jnp.max(held, axis=0, keepdims=True)) * scale))
            return carry

        lax.fori_loop(0, HEADS, heads, 0)

    tiles, dates, strip, _ = encoded_ref.shape
    first = 0
    step = tiles * dates * strip // 4
    for held_ref in x_refs:
        for row in range(0, held_ref.shape[0], step):
            held = held_ref[row : row + step, :].astype(f32) + loc_ref[...]
            updated = held + mm(mixed_ref[:, first : first + step], out_ref[...], TN)
            encoded = layer_norm(updated, final_ref[...].astype(f32)).astype(bf16)
            part = step // (dates * strip)
            group = first // (dates * strip)
            encoded_ref[group : group + part] = encoded.reshape(part, dates, strip, width)
            first += step
    total = bias_ref[...].astype(f32)
    for m in range(dates):
        total = total + mm(encoded_ref[:, m].reshape(tiles * strip, width), wr_ref[place_ref[0] ^ m])
    total = 0.5 * total * (1.0 + lax.erf(total * math.sqrt(0.5)))
    halves = range(reduced_ref.shape[0])
    for s in range(tiles):
        spot = pl.multiple_of((place_ref[1] ^ s) * strip, strip)
        for half in halves:
            lanes = slice(128 * half, 128 * (half + 1))
            reduced_ref[half, pl.ds(spot, strip), :] = total[s * strip : (s + 1) * strip, lanes]
    for half in halves:
        o_ref[:, 128 * half : 128 * (half + 1)] = reduced_ref[half].astype(bf16)

    def column(b):
        return jnp.concatenate([reduced_ref[half, pl.ds(b, PATCHES, stride=PATCHES), :] for half in halves], axis=1)

    tail = jnp.zeros((PATCHES - 2, o_ref.shape[1]), f32)
    tail = jnp.concatenate([profile_ref[...].astype(f32), tail], axis=0)
    is_last = place_ref[2] == 1
    sent = [jnp.where(is_last, column(PATCHES - 2 + i), column(i)) for i in range(2)]
    last_ref[...] = jnp.concatenate(sent + [tail], axis=0).astype(bf16)
    first_ref[...] = jnp.concatenate([column(0), column(1), tail], axis=0).astype(bf16)


def encode(
    place, packed, norms, x, location, out_weight, final_gain, reduce_weight, reduce_bias, profile, tiles, dates
):
    width = out_weight.shape[0]
    tokens = sum(part.shape[0] for part in x)
    strip = tokens // (tiles * dates)
    dec = reduce_weight.shape[1]
    patches = tiles * strip
    sent = jax.ShapeDtypeStruct((3 * PATCHES, dec), bf16)
    whole = pl.BlockSpec(memory_space=pltpu.VMEM)
    return pl.pallas_call(
        functools.partial(encode_kernel, len(packed)),
        in_specs=[pl.BlockSpec(memory_space=pltpu.SMEM)] + [whole] * (3 * len(packed) + 6),
        out_specs=[whole] * 3,
        out_shape=[jax.ShapeDtypeStruct((patches, dec), bf16), sent, sent],
        scratch_shapes=[
            pltpu.VMEM((width, tokens), bf16),
            pltpu.VMEM((tiles, dates, strip, width), bf16),
            pltpu.VMEM((dec // 128, patches, 128), f32),
        ],
        compiler_params=pltpu.CompilerParams(vmem_limit_bytes=28 * 2**20),
        name="encode",
    )(
        place, *packed, *norms, *x, location, out_weight, final_gain,
        reduce_weight.reshape(dates, width, dec), reduce_bias, profile,
    )


FIRST_OWN = RIM // PATCH
LAST_OWN = PATCHES - 1 - FIRST_OWN
UPPER = [a for a in range(PATCHES) if PATCH * a + PATCH >= TILE_PX - RIM]
LOWER = [a for a in range(PATCHES) if PATCH * a - 1 < RIM]
ENTRIES = (
    [(0, a) for a in UPPER]
    + [(0, None)]
    + [(1, a) for a in range(FIRST_OWN, LAST_OWN + 1)]
    + [(2, a) for a in LOWER]
    + [(2, None)]
)
SIDE = 16


def placement():
    main = np.zeros((3, SPAN, PATCHES, STRIDE), np.float32)
    side = np.zeros((3, SIDE, STRIDE), np.float32)
    for j in range(SPAN):
        for slot in range(PATCHES):
            if slot == 0:
                which, x = 0, PATCH * (PATCHES - 1) + j - 1
            elif slot == PATCHES - 1:
                which, x = 2, j - 1
            else:
                which, x = 1, PATCH * slot + j - 1
            column = x + (which - 1) * STRIDE - RIM
            if 0 <= x < TILE_PX and 0 <= column < STRIDE:
                main[which, j, slot, column] = 1.0
    rows = []
    for j in range(SPAN):
        x = PATCH * (PATCHES - 2) + j - 1
        if TILE_PX - RIM <= x < TILE_PX:
            side[0, len(rows), x - (TILE_PX - RIM)] = 1.0
            rows.append((0, j))
    for j in range(SPAN):
        x = PATCH + j - 1
        if 0 <= x < RIM:
            side[2, len(rows), STRIDE - RIM + x] = 1.0
            rows.append((2, j))
    side[0, len(rows), RIM - 1] = 1.0
    side[2, len(rows) + 1, STRIDE - RIM] = 1.0
    return main.reshape(3, SPAN * PATCHES, STRIDE), side, rows


PLACE_MAIN, PLACE_SIDE, SIDE_ROWS = placement()


def windows():
    table = np.zeros((3, LANES, STRIDE), np.float32)
    for x in range(STRIDE):
        table[1, x + RIM, x] = 1.0
    for x in range(RIM):
        table[0, TILE_PX - RIM + x, x] = 1.0
        table[2, x, STRIDE - RIM + x] = 1.0
    return table


def row_lanes(classes):
    table = np.zeros((LANES, len(ENTRIES), LANES), np.float32)
    for n, (tile_row, a) in enumerate(ENTRIES):
        for k in range(classes):
            if a is None:
                halo = classes * SPAN + k + (classes if tile_row == 0 else 0)
                table[TILE_PX - 1 if tile_row == 0 else 0, n, halo] = 1.0
                continue
            for i in range(SPAN):
                y = PATCH * a - 1 + i
                if 0 <= y < TILE_PX:
                    table[y, n, k * SPAN + i] = 1.0
    return table.reshape(LANES, -1)


def tap_tables(classes):
    rows = np.zeros((LANES, classes), np.float32)
    columns = np.zeros((FEAT, FEAT * PATCH), np.float32)
    meet = np.zeros((3, LANES, FEAT, PATCH), np.float32)
    for f in range(FEAT):
        columns[f, f * PATCH : (f + 1) * PATCH] = 1.0
    for k in range(classes):
        rows[k * SPAN : (k + 1) * SPAN, k] = 1.0
        rows[classes * SPAN + k, k] = 1.0
        rows[classes * (SPAN + 1) + k, k] = 1.0
        for dy in range(3):
            for i in range(PATCH):
                meet[dy, k * SPAN + i + 2 - dy, :, i] = 1.0
        meet[0, classes * SPAN + k, :, FAR_PIXEL] = 1.0
        meet[2, classes * (SPAN + 1) + k, :, NEAR_PIXEL] = 1.0
    return rows, columns, meet.reshape(3, LANES, FEAT * PATCH)


def prepare_kernel(
    up_ref, taps_ref, rows_ref, columns_ref, meet_ref, weight_ref,
    o_ref, edge_ref, held_ref, turned_ref, column_ref, sem
):
    load = pltpu.make_async_copy(weight_ref, held_ref, sem)
    load.start()
    for half in range(turned_ref.shape[0]):
        lanes = slice(128 * half, 128 * (half + 1))
        turned_ref[half] = up_ref[lanes, :].astype(f32).T
        for j in range(PATCH):
            column_ref[j, :, lanes] = turned_ref[half, pl.ds(j, FEAT * PATCH, stride=PATCH), :].astype(bf16)
    spread = []
    for dx in range(3):
        total = None
        for dy in range(3):
            taps = mm(mm(rows_ref[...], taps_ref[3 * dy + dx]).astype(bf16), columns_ref[...])
            part = taps * meet_ref[dy].astype(f32)
            total = part if total is None else total + part
        spread.append(total.astype(bf16))
    for big in range(SPAN):
        total = None
        for dx in range(3):
            j = big - 2 + dx
            if 0 <= j < PATCH:
                part = mm(spread[dx], column_ref[j])
                total = part if total is None else total + part
        o_ref[big] = total.astype(bf16)
    edge_ref[0] = mm(spread[2], column_ref[NEAR_PIXEL]).astype(bf16)
    edge_ref[1] = mm(spread[0], column_ref[FAR_PIXEL]).astype(bf16)
    load.wait()


def prepare_weights(upsample_weight, class_weight, qkv_weight):
    channels = upsample_weight.shape[0]
    tables = [jnp.asarray(table, bf16) for table in tap_tables(class_weight.shape[1])]
    whole = pl.BlockSpec(memory_space=pltpu.VMEM)
    return pl.pallas_call(
        prepare_kernel,
        in_specs=[whole] * 5 + [pl.BlockSpec(memory_space=pltpu.HBM)],
        out_specs=[whole] * 3,
        out_shape=[
            jax.ShapeDtypeStruct((SPAN, LANES, channels), bf16),
            jax.ShapeDtypeStruct((2, LANES, channels), bf16),
            pltpu.VMEM(qkv_weight.shape, bf16),
        ],
        scratch_shapes=[
            pltpu.VMEM((channels // 128, upsample_weight.shape[1], 128), f32),
            pltpu.VMEM((PATCH, FEAT * PATCH, channels), bf16),
            pltpu.SemaphoreType.DMA,
        ],
        compiler_params=pltpu.CompilerParams(vmem_limit_bytes=24 * 2**20),
        cost_estimate=pl.CostEstimate(flops=0, bytes_accessed=0, transcendentals=0),
        name="prepare_weights",
    )(upsample_weight, class_weight, *tables, pltpu.with_memory_space_constraint(qkv_weight, pltpu.HBM))


def compose_kernel(
    classes, own_ref, before_ref, after_ref, above_ref, below_ref, profile_ref, m_ref, edge_ref,
    lanes_ref, window_ref, place_ref, side_ref, bias_ref,
    o_ref, a_ref, b_ref, z_ref, z2_ref, acc_ref, out_ref, sems
):
    count = len(ENTRIES)
    edge = len(UPPER)
    own, before, after, above, below = (
        ref[...].astype(f32) for ref in (own_ref, before_ref, after_ref, above_ref, below_ref)
    )
    slot = lax.broadcasted_iota(jnp.int32, (PATCHES, LANES), 0)

    def line(tile_row, a):
        if tile_row == 1 or a is None:
            a = a if a is not None else (NEAR_PATCH if tile_row == 0 else FAR_PATCH)
            sides = [before[a : a + 1], before[PATCHES + a : PATCHES + a + 1]]
            sides += [after[a : a + 1], after[PATCHES + a : PATCHES + a + 1]]
            return own[PATCHES * a : PATCHES * (a + 1)], sides
        source = above if tile_row == 0 else below
        n = (UPPER if tile_row == 0 else LOWER).index(a)
        first = PATCHES * edge + 4 * n
        return source[PATCHES * n : PATCHES * (n + 1)], [source[first + i : first + i + 1] for i in range(4)]

    def slots(rows, base):
        for i, row in rows.items():
            base = jnp.where(slot == i, row, base)
        return base

    def second(before_row, after_row, near, far):
        rows = {i: before_row if which == 0 else after_row for i, (which, _) in enumerate(SIDE_ROWS)}
        rows[len(SIDE_ROWS)] = near
        rows[len(SIDE_ROWS) + 1] = far
        return slots(rows, jnp.zeros((SIDE, LANES), f32))

    profile = profile_ref[...].astype(f32)
    tail = slice(2 * PATCHES, 2 * PATCHES + 2)
    ends = slice((PATCHES + 4) * edge, (PATCHES + 4) * edge + 6)
    profiles = jnp.concatenate([above[ends], before[tail], profile, after[tail], below[ends]], axis=0)
    row_profiles = [profiles[2 * i : 2 * i + 1] for i in range(9)]
    col_profiles = [profiles[2 * i + 1 : 2 * i + 2] for i in range(9)]
    blank = jnp.zeros((PATCHES - 9, LANES), f32)
    row_table = jnp.concatenate(row_profiles + [blank], axis=0).astype(bf16)
    col_table = jnp.concatenate(col_profiles + [blank], axis=0).astype(bf16)
    weights = mm(row_table, lanes_ref[...])
    rows = [mm(row_table, window_ref[i]) for i in range(3)]
    cols = [mm(col_table, window_ref[i]) for i in range(3)]
    block_rows = jnp.concatenate([rows[i // 3][i : i + 1] for i in range(9)] + [blank[:, :STRIDE]], axis=0)
    block_cols = jnp.concatenate([cols[i % 3][i : i + 1] for i in range(9)] + [blank[:, :STRIDE]], axis=0)
    den = mm(block_rows.astype(bf16), block_cols.astype(bf16), TN)
    spots, side_spots = [], []
    for tile_row in range(3):
        spots.append(sum(place_ref[i].astype(f32) * block_cols[3 * tile_row + i][None] for i in range(3)).astype(bf16))
        side_spots.append(
            sum(side_ref[i].astype(f32) * block_cols[3 * tile_row + i][None] for i in range(3)).astype(bf16)
        )

    def entry_weights(n, tile_row):
        return [weights[3 * tile_row + i : 3 * tile_row + i + 1, LANES * n : LANES * (n + 1)] for i in range(3)]

    main_weights, side_weights = [], []
    for n, (tile_row, a) in enumerate(ENTRIES):
        patches, (l_far, l_near, r_near, r_far) = line(tile_row, a)
        a_ref[n] = slots({0: l_near, PATCHES - 1: r_near}, patches).astype(bf16)
        b_ref[n] = second(
            l_far, r_far, patches[NEAR_PATCH : NEAR_PATCH + 1], patches[FAR_PATCH : FAR_PATCH + 1]
        ).astype(bf16)
        left, middle, right = entry_weights(n, tile_row)
        main_weights.append(slots({0: left, PATCHES - 1: right}, jnp.broadcast_to(middle, (PATCHES, LANES))))
        side_weights.append(second(left, right, left, right))
    main_weights = jnp.stack(main_weights)
    for j in range(SPAN):
        z = mm(a_ref[...].reshape(count * PATCHES, LANES), m_ref[j], NT).reshape(count, PATCHES, LANES)
        z_ref[:, j] = (z * main_weights).astype(bf16)
    side_slot = lax.broadcasted_iota(jnp.int32, (count, SIDE, LANES), 1)
    patches = b_ref[...].astype(f32)
    total = None
    for i in range(len(SIDE_ROWS) + 2):
        kernel = m_ref[SIDE_ROWS[i][1]] if i < len(SIDE_ROWS) else edge_ref[i - len(SIDE_ROWS)]
        part = jnp.where(side_slot == i, patches, 0.0).astype(bf16).reshape(count * SIDE, LANES)
        part = mm(part, kernel, NT)
        total = part if total is None else total + part
    z2_ref[...] = (total.reshape(count, SIDE, LANES) * jnp.stack(side_weights)).astype(bf16)

    acc_ref[...] = jnp.zeros_like(acc_ref)
    inverse = 1.0 / jnp.maximum(den, 1.0)
    step = STRIDE // sems.shape[0]
    copies = []

    def finish():
        first = len(copies) * step
        rows = slice(first, first + step)
        for k in range(classes):
            total = acc_ref[k, RIM + first : RIM + first + step, :] + bias_ref[k] * den[rows]
            out_ref[k, rows, :] = total * inverse[rows]
        copies.append(pltpu.make_async_copy(out_ref.at[:, rows, :], o_ref.at[:, rows, :], sems.at[len(copies)]))
        copies[-1].start()

    for n, (tile_row, a) in enumerate(ENTRIES):
        part = mm(z_ref[n].reshape(SPAN * PATCHES, LANES), spots[tile_row], TN)
        part += mm(z2_ref[n], side_spots[tile_row], TN)
        if a is None:
            first = classes * SPAN + (classes if tile_row == 0 else 0)
            y = 2 * RIM - 1 if tile_row == 0 else STRIDE
            for k in range(classes):
                acc_ref[k, y : y + 1, :] += part[first + k : first + k + 1]
            continue
        y = PATCH * a - 1 + (tile_row - 1) * STRIDE
        low, high = 0, SPAN
        if tile_row == 0:
            high = min(SPAN, TILE_PX - (PATCH * a - 1))
        if tile_row == 2:
            low = max(0, 1 - PATCH * a)
        for k in range(classes):
            acc_ref[k, y + low : y + high, :] += part[k * SPAN + low : k * SPAN + high]
        if tile_row == 1:
            clear = min(y + PATCH, STRIDE) - RIM
            while (len(copies) + 1) * step <= clear and len(copies) + 1 < sems.shape[0]:
                finish()
    while len(copies) < sems.shape[0]:
        finish()
    for copy in copies:
        copy.wait()


def forward(size):
    return [(i, i + 1) for i in range(size - 1)]


def backward(size):
    return [(i + 1, i) for i in range(size - 1)]


def forward(size):
    return [(i, i + 1) for i in range(size - 1)]


def backward(size):
    return [(i + 1, i) for i in range(size - 1)]


def exchange_rims(reduced, last, first, profile):
    cols = lax.axis_size("col")
    if cols == 2:
        other = swap(last, "col", 1)
        at_end = lax.axis_index("col") == 1
        before, after = jnp.where(at_end, other, 0), jnp.where(at_end, 0, other)
    else:
        before = lax.ppermute(last, "col", forward(cols))
        after = lax.ppermute(first, "col", backward(cols))

    def lines(rows):
        parts = [reduced[PATCHES * a : PATCHES * (a + 1)] for a in rows]
        for a in rows:
            for side in (before, after):
                parts += [side[a : a + 1], side[PATCHES + a : PATCHES + a + 1]]
        parts += [before[2 * PATCHES : 2 * PATCHES + 2], profile, after[2 * PATCHES : 2 * PATCHES + 2]]
        used = (PATCHES + 4) * len(rows) + 6
        parts.append(jnp.zeros((-used % 16, reduced.shape[1]), bf16))
        return jnp.concatenate(parts, axis=0)

    rows = lax.axis_size("date") * lax.axis_size("tile")
    above = lax.ppermute(lines(UPPER), ("date", "tile"), forward(rows))
    below = lax.ppermute(lines(LOWER), ("date", "tile"), backward(rows))
    return before, after, above, below


def compose(reduced, rims, profile, kernels, edges, class_bias, classes):
    channels = reduced.shape[1]
    count = len(ENTRIES)
    whole = pl.BlockSpec(memory_space=pltpu.VMEM)
    tables = [jnp.asarray(t, bf16) for t in (row_lanes(classes), windows(), PLACE_MAIN, PLACE_SIDE)]
    return pl.pallas_call(
        functools.partial(compose_kernel, classes),
        in_specs=[whole] * 12 + [pl.BlockSpec(memory_space=pltpu.SMEM)],
        out_specs=pl.BlockSpec(memory_space=pl.ANY),
        out_shape=jax.ShapeDtypeStruct((classes, STRIDE, STRIDE), f32),
        scratch_shapes=[
            pltpu.VMEM((count, PATCHES, channels), bf16),
            pltpu.VMEM((count, SIDE, channels), bf16),
            pltpu.VMEM((count, SPAN, PATCHES, LANES), bf16),
            pltpu.VMEM((count, SIDE, LANES), bf16),
            pltpu.VMEM((classes, TILE_PX, STRIDE), f32),
            pltpu.VMEM((classes, STRIDE, STRIDE), f32),
            pltpu.SemaphoreType.DMA((4,)),
        ],
        compiler_params=pltpu.CompilerParams(vmem_limit_bytes=52 * 2**20),
        name="compose",
    )(reduced, *rims, profile, kernels, edges, *tables, class_bias.astype(f32))


def local(
    arrivals,
    owner_map,
    block_ids,
    tile_valid,
    blend_weights,
    location_table,
    norm_gain,
    qkv_weight,
    out_weight,
    final_gain,
    reduce_weight,
    reduce_bias,
    upsample_weight,
    class_weight,
    class_bias,
):
    width = arrivals.shape[-1]
    slots = arrivals.shape[1]
    classes = class_weight.shape[1]
    dates, tiles = lax.axis_size("date"), lax.axis_size("tile")
    codes = block_ids.reshape(1, 1)
    one_hot = (codes == jnp.arange(location_table.shape[0], dtype=jnp.int32)[None, :]).astype(bf16)

    def prepare(stacked):
        table, blend, up, _ = lax.optimization_barrier((location_table, blend_weights, upsample_weight, stacked))
        location = jnp.dot(one_hot, table, preferred_element_type=f32)
        profile = blend.reshape(2, TILE_PX).astype(bf16)
        profile = jnp.concatenate([profile[:1] * tile_valid.reshape(1).astype(bf16), profile[1:]], axis=0)
        profile = jnp.pad(profile, ((0, 0), (0, LANES - TILE_PX)))
        kernels, edges, held_weight = prepare_weights(up, class_weight, qkv_weight)
        return edges, location, profile, kernels, held_weight

    def use(pieces, prepared):
        return project(pieces, prepared[1], norm_gain[None], prepared[4])

    (packed, norms, x), prepared = exchange(arrivals.reshape(slots, -1, width), owner_map[0], prepare, use)
    edges, location, profile, kernels, _ = prepared
    go_last = jnp.where((lax.axis_index("col") == 0) | (lax.axis_size("col") != 2), 1, 0)
    place = jnp.stack([lax.axis_index("date"), lax.axis_index("tile"), go_last]).astype(jnp.int32)
    reduced, to_after, to_before = encode(
        place, packed, norms, x, location, out_weight, final_gain[None], reduce_weight, reduce_bias[None], profile,
        tiles, dates
    )
    rims = exchange_rims(reduced, to_after, to_before, profile)
    return compose(reduced, rims, profile, kernels, edges, class_bias, classes)[None]


def solution(mesh):
    placed = (
        P(None, None, "col", "date", "tile", None, None),
        P(),
        P(None, ("date", "tile"), "col"),
        P(None, ("date", "tile"), "col"),
        P(None, ("date", "tile"), "col", None, None),
    ) + (P(),) * 10
    return jax.shard_map(
        local,
        mesh=mesh,
        in_specs=placed,
        out_specs=P(None, None, ("date", "tile"), "col"),
        check_vma=False,
    )
```
